32 devices in a mesh: groups: 2 (over y), ctx: 8 (over z, x), head: 2 (over core).
Axes of the slice: x: 2, y: 2, z: 4, core: 2. Of those that a mesh axis runs over, the one named last changes fastest.
Arguments:
- queries: bfloat16 [4096, 2, 256], P(('groups', 'ctx'), 'head'), parts along dimension 0, may hold values from -6 to 6
- keys: bfloat16 [4096, 2, 256], P(('groups', 'ctx'), 'head'), parts along dimension 0, may hold values from -6 to 6
- values: bfloat16 [4096, 2, 256], P(('groups', 'ctx'), 'head'), parts along dimension 0, may hold values from -6 to 6
- lambda_vectors: float32 [4, 2, 128], P(None, 'head'), may hold values from -1.2 to 1.2
- out_weight: bfloat16 [8192, 512], P('ctx', 'head'), may hold values from -0.25 to 0.25
- local_len: int32 [32], P(('groups', 'ctx')), parts along dimension 0, may hold values from 1 to 3
- stride_keys: int32 [32, 3], P(('groups', 'ctx')), parts along dimension 0, may hold values from -1 to 11, as said below
- global_blocks: int32 [8], P('groups'), parts along dimension 0, may hold values from 0 to 15, as said below
Outputs:
- layer_out: bfloat16 [4096, 8192], P(('groups', 'ctx'), 'head'), parts along dimension 0
The draws below stay inside these ranges and needn't reach their ends.
There are 2 independent parts, one for each index of `groups`. The reference program is written for one: setup_inputs(seed, part) draws one part's arguments, and reference() takes and returns one part's arrays. A program takes and returns all parts, laid end to end along the dimension named above; an argument that names none is the same for every part. Nothing has to cross between parts.
Inputs may be any that keep to these rules, and one draw needn't show every extreme that they name: `stride_keys`: entry j of query block b is either b - (j + 1) * 4 or -1, and -1 where that would be negative. `global_blocks`: 4 distinct block indices.
All inputs are finite; a program needn't handle non-finite values.
Results may differ from the reference program's by a relative error of at most 0.001.
The reference program's roundings to bfloat16 on the way count: a program that leaves them out, or rounds other values in their place, can miss the bound.
Values may be sent and summed in bfloat16 or wider, within the bound.
A program may use at most 64 MiB of HBM per device.

```python
import math
import jax
import jax.numpy as jnp
from jax import lax

D = 8192
DH = 128
HEADS_DEV = 1
BLK = 128
LOCAL = 3
NSTR = 3
GLOB = 4
LAYER = 12
HEADS = 2
TOKENS = 2048
NB = 16
STRIDE = 4
N_HEAD = 2


def draw_queries(key, part):
    key = jax.random.fold_in(key, 11)
    sample = jnp.clip(jax.random.normal(key, (TOKENS, HEADS, 2 * DH), jnp.float32), -6.0, 6.0)
    return sample.astype(jnp.bfloat16)


def draw_keys(key, part):
    key = jax.random.fold_in(key, 12)
    sample = jnp.clip(jax.random.normal(key, (TOKENS, HEADS, 2 * DH), jnp.float32), -6.0, 6.0)
    return sample.astype(jnp.bfloat16)


def draw_stride_keys(key, part):
    key = jax.random.fold_in(key, 21)
    query_block = jnp.arange(NB, dtype=jnp.int32)[:, None]
    slot_pos = jnp.arange(NSTR, dtype=jnp.int32)[None, :]
    target = query_block - (slot_pos + 1) * STRIDE
    coin_flip = jax.random.randint(key, (NB, NSTR), 0, 2).astype(jnp.int32)
    coin_flip = coin_flip.at[NB - 1, 0].set(1)
    return jnp.where((target >= 0) & (coin_flip == 1), target, -1).astype(jnp.int32)


def draw_global_blocks(key, part):
    key = jax.random.fold_in(key, 22)
    return jax.random.permutation(key, NB)[:GLOB].astype(jnp.int32)


def place_ends(drawn, stream_key, least, top_value):
    extent = drawn.shape
    place = [jax.random.randint(jax.random.fold_in(stream_key, axis), (), 0, extent[axis]) for axis in range(len(extent))]
    drawn = drawn.at[tuple(place)].set(least)
    longest = extent.index(max(extent))
    place[longest] = (place[longest] + 1) % extent[longest]
    return drawn.at[tuple(place)].set(top_value)


def shard_levels(key, shape, pieces, smallest, top_value):
    gain = 1.0
    for axis_at, shards_of in pieces:
        draws = jax.random.uniform(jax.random.fold_in(jax.random.fold_in(key, 6), axis_at), (shards_of,), jnp.float32, smallest / len(pieces), top_value / len(pieces))
        gain = gain * jnp.repeat(jnp.exp(draws), shape[axis_at] // shards_of).reshape((-1,) + (1,) * (len(shape) - 1 - axis_at))
    return gain


def scatter_about(stream_key, shape, scale, most, cuts=(), kind=jnp.bfloat16):
    array = jax.random.normal(stream_key, shape, jnp.float32) * scale
    if len(cuts) > 0:
        array = shard_levels(stream_key, shape, cuts, -0.22, 0.18) * array
    return jnp.clip(array, min=-most, max=most).astype(kind)


def setup_inputs(seed: int = 0, part: int = 0) -> dict:
    key_list = jax.random.split(jax.random.key(seed), 9)
    part_keys = jax.random.split(jax.random.fold_in(key_list[8], part), 9)
    queries = draw_queries(jax.random.fold_in(jax.random.fold_in(key_list[8], part), 71), part)
    keys = draw_keys(jax.random.fold_in(jax.random.fold_in(key_list[8], part), 71), part)
    values = scatter_about(part_keys[2], (TOKENS, HEADS, 2 * DH), 1.0, 6.0, ((0, 8), (1, 2)))
    lambda_vectors = scatter_about(key_list[3], (4, HEADS, DH), 0.2, 1.2, ((1, 2),), jnp.float32)
    out_weight = scatter_about(key_list[4], (D, HEADS * 2 * DH), (HEADS * 2 * DH) ** -0.5, 0.25, ((0, 8), (1, 2)))
    local_len = place_ends(jax.random.randint(part_keys[5], (NB,), 1, LOCAL + 1), jax.random.fold_in(part_keys[5], 1), 1, LOCAL).astype(jnp.int32)
    stride_keys = draw_stride_keys(jax.random.fold_in(jax.random.fold_in(key_list[8], part), 71), part)
    global_blocks = draw_global_blocks(jax.random.fold_in(jax.random.fold_in(key_list[8], part), 71), part)
    return {"queries": queries, "keys": keys, "values": values, "lambda_vectors": lambda_vectors, "out_weight": out_weight, "local_len": local_len, "stride_keys": stride_keys, "global_blocks": global_blocks}


def masked_softmax(scores, allowed):
    masked_scores = jnp.where(allowed, scores, -jnp.inf)
    highest = lax.optimization_barrier(jnp.max(masked_scores, -1, keepdims=True))
    raised = jnp.where(allowed, jnp.exp(masked_scores - highest), 0.0)
    return raised / lax.optimization_barrier(jnp.sum(raised, -1, keepdims=True))

def reference(queries, keys, values, lambda_vectors, out_weight, local_len, stride_keys, global_blocks):
    lam_init = 0.8 - 0.6 * math.exp(-0.3 * (LAYER - 1))
    vectors = lambda_vectors.astype(jnp.float32)
    mixing = jnp.exp(lax.optimization_barrier(jnp.sum(vectors[0] * vectors[1], -1))) - jnp.exp(lax.optimization_barrier(jnp.sum(vectors[2] * vectors[3], -1))) + lam_init
    double_width = 2 * DH
    query_all = queries.reshape(NB, BLK, HEADS, double_width)
    key_all = keys.reshape(NB, BLK, HEADS, double_width)
    value_all = values.reshape(NB, BLK, HEADS, double_width)
    score_scale = 1.0 / math.sqrt(DH)
    offsets = jnp.arange(LOCAL, dtype=jnp.int32) - (LOCAL - 1)
    inside = jnp.arange(BLK, dtype=jnp.int32)

    def one_block(query_block):
        window_floor = query_block - local_len[query_block]
        local_ids = query_block + offsets
        local_ok = (local_ids > window_floor) & (local_ids >= 0)
        stride_ids = stride_keys[query_block]
        stride_ok = stride_ids >= 0
        seen = jnp.any(global_blocks[:, None] == stride_ids[None, :], axis=1)
        global_ok = (global_blocks <= window_floor) & jnp.logical_not(seen)
        block_ids = jnp.concatenate([local_ids, stride_ids, global_blocks]).astype(jnp.int32)
        block_ok = jnp.concatenate([local_ok, stride_ok, global_ok])
        block_count = block_ids.shape[0]
        safe_ids = jnp.clip(block_ids, 0, NB - 1)
        key_rows = key_all[safe_ids].reshape(block_count * BLK, HEADS, double_width).astype(jnp.float32)
        value_rows = value_all[safe_ids].reshape(block_count * BLK, HEADS, double_width).astype(jnp.float32)
        self_key = jnp.repeat(block_ids == query_block, BLK)
        key_inside = jnp.tile(inside, block_count)
        allowed = jnp.repeat(block_ok, BLK)[None, :] & (jnp.logical_not(self_key)[None, :] | (key_inside[None, :] <= inside[:, None]))
        query_rows = query_all[query_block].astype(jnp.float32)
        scores_one = jnp.einsum('qhd,khd->hqk', query_rows[..., :DH], key_rows[..., :DH]) * score_scale
        scores_two = jnp.einsum('qhd,khd->hqk', query_rows[..., DH:], key_rows[..., DH:]) * score_scale
        attn_one = masked_softmax(scores_one, allowed)
        attn_two = masked_softmax(scores_two, allowed)
        weights = (attn_one - mixing[:, None, None] * attn_two).astype(jnp.bfloat16)
        mixed_out = jnp.einsum('hqk,khe->qhe', weights.astype(jnp.float32), value_rows)
        normed = mixed_out * lax.rsqrt(lax.optimization_barrier(jnp.mean(mixed_out * mixed_out, -1, keepdims=True)) + 1e-05) * (1.0 - lam_init)
        return normed.astype(jnp.bfloat16)
    normed = lax.map(one_block, jnp.arange(NB, dtype=jnp.int32)).reshape(TOKENS, HEADS * double_width)
    columns = HEADS_DEV * double_width
    summed = jnp.zeros((TOKENS, D), jnp.float32)
    for group_pos in range(N_HEAD):
        partial_value = jnp.dot(normed[:, group_pos * columns:(group_pos + 1) * columns], out_weight[:, group_pos * columns:(group_pos + 1) * columns].T, preferred_element_type=jnp.float32)
        partial_value = lax.optimization_barrier(partial_value.astype(jnp.bfloat16))
        summed = summed + partial_value.astype(jnp.float32)
    return summed.astype(jnp.bfloat16)
```

```python
import functools
import math

import jax
import jax.numpy as jnp
from jax import lax
from jax.experimental import pallas as pl
from jax.experimental.pallas import tpu as pltpu
from jax.sharding import PartitionSpec as P

BLK = 128
NSTR = 3
GLOB = 4
LAYER = 12


def shifted(shard, axis, by):
    length = lax.axis_size(axis)
    pairs = [(i, i + by) for i in range(length) if 0 <= i + by < length]
    return lax.ppermute(shard, axis, pairs)


def from_root(value, axis, source):
    kept = jnp.where(lax.axis_index(axis) == source, value, 0).astype(value.dtype)
    return lax.psum(kept, axis)


def masked_softmax(scores, allowed):
    masked_scores = jnp.where(allowed, scores, -jnp.inf)
    highest = jnp.max(masked_scores, -1, keepdims=True)
    raised = jnp.where(allowed, jnp.exp(masked_scores - highest), 0.0)
    return raised / jnp.sum(raised, -1, keepdims=True)


def body(queries, keys, values, lambda_vectors, out_weight, local_len, stride_keys, global_blocks):
    tok_dev, heads_here, double_width = queries.shape
    head_dim = double_width // 2
    blocks_here = tok_dev // BLK
    ctx_count = lax.axis_size("ctx")
    ctx_pos = lax.axis_index("ctx")
    step_dev = ctx_count // (NSTR + 1)
    lam_init = 0.8 - 0.6 * math.exp(-0.3 * (LAYER - 1))
    mixing = (
        jnp.exp(jnp.sum(lambda_vectors[0] * lambda_vectors[1], -1))
        - jnp.exp(jnp.sum(lambda_vectors[2] * lambda_vectors[3], -1))
        + lam_init
    )
    key_vals = jnp.concatenate((keys, values), axis=-1)
    prev_data = shifted(key_vals, "ctx", 1)
    remote = []
    moving = key_vals
    for slot_pos in range(NSTR):
        moving = shifted(moving, "ctx", step_dev)
        remote.append(moving)
    global_list = []
    for global_pos in range(GLOB):
        block_id = global_blocks[global_pos]
        owner_pos = block_id // blocks_here
        first_row = block_id % blocks_here * BLK
        block_data = lax.dynamic_slice_in_dim(key_vals, first_row, BLK, 0)
        global_list.append(from_root(block_data, "ctx", owner_pos))
    global_data = jnp.concatenate(global_list, 0)
    candidates = jnp.concatenate([key_vals, prev_data] + remote + [global_data], 0)
    cand_keys = candidates[..., :double_width]
    cand_values = candidates[..., double_width:]
    rows_here = jnp.arange(tok_dev, dtype=jnp.int32)
    query_pos = ctx_pos * tok_dev + rows_here
    query_block = query_pos // BLK
    owner_mask = (rows_here // BLK)[:, None] == jnp.arange(blocks_here, dtype=jnp.int32)[None, :]
    length = jnp.sum(jnp.where(owner_mask, local_len[None, :], 0), 1)
    stride_rows = jnp.sum(jnp.where(owner_mask[:, :, None], stride_keys[None, :, :], 0), 1)
    window_floor = query_block - length
    own_block = ctx_pos * blocks_here + rows_here // BLK
    own_ok = (own_block[None, :] > window_floor[:, None]) & (
        query_pos[None, :] - rows_here[:, None] + rows_here[None, :] <= query_pos[:, None]
    )
    prev_block = (ctx_pos - 1) * blocks_here + rows_here // BLK
    prev_ok = (prev_block[None, :] > window_floor[:, None]) & (prev_block[None, :] >= 0)
    masks = [own_ok, prev_ok]
    for slot_pos in range(NSTR):
        far_block = (ctx_pos - (slot_pos + 1) * step_dev) * blocks_here + rows_here // BLK
        listed = stride_rows[:, slot_pos][:, None]
        masks.append((listed == far_block[None, :]) & (listed >= 0))
    in_stride = jnp.any(stride_rows[:, :, None] == global_blocks[None, None, :], 1)
    global_key = jnp.repeat(global_blocks, BLK)
    global_ok = (global_key[None, :] <= window_floor[:, None]) & jnp.logical_not(
        jnp.repeat(in_stride, BLK, axis=1)
    )
    masks.append(global_ok)
    allowed = jnp.concatenate(masks, 1)
    score_scale = 1.0 / math.sqrt(head_dim)
    scores_one = (
        jnp.einsum(
            "qhd,khd->hqk",
            queries[..., :head_dim],
            cand_keys[..., :head_dim],
            preferred_element_type=jnp.float32,
        )
        * score_scale
    )
    scores_two = (
        jnp.einsum(
            "qhd,khd->hqk",
            queries[..., head_dim:],
            cand_keys[..., head_dim:],
            preferred_element_type=jnp.float32,
        )
        * score_scale
    )
    attn_one = masked_softmax(scores_one, allowed)
    attn_two = masked_softmax(scores_two, allowed)
    weights = (attn_one - mixing[:, None, None] * attn_two).astype(jnp.bfloat16)
    mixed_out = jnp.einsum("hqk,khe->qhe", weights, cand_values, preferred_element_type=jnp.float32)
    normed = (
        mixed_out
        * lax.rsqrt(jnp.mean(mixed_out * mixed_out, -1, keepdims=True) + 1e-05)
        * (1.0 - lam_init)
    ).astype(jnp.bfloat16)
    flat_heads = normed.reshape(tok_dev, heads_here * double_width)
    partials = lax.dot_general(
        flat_heads,
        lax.all_gather(out_weight, "ctx", axis=0, tiled=True),
        (((1,), (1,)), ((), ())),
        preferred_element_type=jnp.float32,
    )
    return lax.psum_scatter(partials.astype(jnp.bfloat16), "head", scatter_dimension=1, tiled=True)


MESH_ID = pl.DeviceIdType.MESH
MASKED = -1e30


def kernel(
    n, q_ref, k_ref, v_ref, w_ref, lam_ref, len_ref, stride_ref, glob_ref, out_ref,
    kv, wown, wother, scores, probs, mine, theirs, obuf,
    kvu_s, kvx_s, kv_r, wu_s, wd_s, wx_s, w_r, wy_s, wy_r, sw_s, sw_r, nm_s, nm_r, loc, out_s,
):
    tok, width = q_ref.shape
    dh = width // 2
    rows = w_ref.shape[0]
    half = rows // 2
    nz, nh = n // 2, n // 2
    y, c, h = lax.axis_index("groups"), lax.axis_index("ctx"), lax.axis_index("head")
    z, x = c // 2, c % 2
    has_up, has_down = z + 1 < nz, z >= 1
    up, down, side = {"ctx": c + 2}, {"ctx": c - 2}, {"ctx": c + 1 - 2 * x}
    twin, core = {"groups": 1 - y}, {"head": 1 - h}
    lo = pl.multiple_of(y * half, half)
    hi = pl.multiple_of((1 - y) * half, half)

    barrier = pltpu.get_barrier_semaphore()
    for to in (side, twin, core):
        pl.semaphore_signal(barrier, inc=1, device_id=to, device_id_type=MESH_ID)

    @pl.when(has_up)
    def _():
        pl.semaphore_signal(barrier, inc=1, device_id=up, device_id_type=MESH_ID)

    @pl.when(has_down)
    def _():
        pl.semaphore_signal(barrier, inc=1, device_id=down, device_id_type=MESH_ID)

    load = pltpu.make_async_copy(w_ref, wown.at[c], loc)
    load.start()
    kv[c, 0] = k_ref[...]
    kv[c, 1] = v_ref[...]
    pl.semaphore_wait(barrier, 3 + has_up.astype(jnp.int32) + has_down.astype(jnp.int32))

    def remote(src, dst, send, recv, to):
        return pltpu.make_async_remote_copy(
            src_ref=src, dst_ref=dst, send_sem=send, recv_sem=recv, device_id=to, device_id_type=MESH_ID
        )

    def kv_copy(b, send, to):
        return remote(kv.at[b], kv.at[b], send.at[b], kv_r.at[b], to)

    def w_copy(b, send, to):
        piece = wown.at[b, pl.ds(lo, half)]
        return remote(piece, piece, send.at[b], w_r.at[b], to)

    def y_copy(b, start):
        piece = wown.at[b, pl.ds(start, half)]
        return remote(piece, piece, wy_s.at[b], wy_r.at[b], twin)

    def swap_copy(b, which):
        start = pl.multiple_of(which * half, half)
        slot = b % nh
        return remote(
            wown.at[b, pl.ds(start, half)], wother.at[slot, pl.ds(start, half)],
            sw_s.at[2 * slot + which], sw_r.at[2 * slot + which], core,
        )

    def swap(b, which):
        @pl.when(b // nh == 1 - h)
        def _():
            swap_copy(b, which).start()

    def kv_up(d):
        @pl.when(z >= d)
        def _():
            b = c - 2 * d
            kv_copy(b, kvu_s, up).wait_recv()

            @pl.when(has_up)
            def _():
                kv_copy(b, kvu_s, up).start()

            kv_copy(b, kvx_s, side).start()

    def w_down(d):
        @pl.when(z + d < nz)
        def _():
            b = c + 2 * d
            w_copy(b, wd_s, down).wait_recv()

            @pl.when(has_down)
            def _():
                w_copy(b, wd_s, down).start()

            y_copy(b, lo).start()
            w_copy(b, wx_s, side).start()
            swap(b, y)

    def w_up(d):
        @pl.when(z >= d)
        def _():
            b = c - 2 * d
            w_copy(b, wu_s, up).wait_recv()

            @pl.when(has_up)
            def _():
                w_copy(b, wu_s, up).start()

            y_copy(b, lo).start()
            w_copy(b, wx_s, side).start()
            swap(b, y)

    def w_side(d):
        @pl.when((z + d < nz) & (z + d >= 0))
        def _():
            b = 2 * (z + d) + 1 - x
            w_copy(b, wx_s, side).wait_recv()
            y_copy(b, lo).start()
            swap(b, y)

    def w_twin(b):
        y_copy(b, hi).wait_recv()
        swap(b, 1 - y)

    def kv_side(d):
        @pl.when((z >= d) & ((d > 0) | (x == 1)))
        def _():
            b = 2 * (z - d) + 1 - x
            kv_copy(b, kvx_s, side).wait_recv()

    @pl.when(has_up)
    def _():
        kv_copy(c, kvu_s, up).start()

    @pl.when(x == 0)
    def _():
        kv_copy(c, kvx_s, side).start()

    load.wait()

    @pl.when(has_down)
    def _():
        w_copy(c, wd_s, down).start()

    w_copy(c, wx_s, side).start()

    @pl.when(has_up)
    def _():
        w_copy(c, wu_s, up).start()

    swap(c, 0)
    swap(c, 1)

    for b in range(1, n):
        @pl.when(c < b)
        def _(b=b):
            kv[b] = jnp.zeros(kv.shape[1:], kv.dtype)

    for d in range(1, nz):
        kv_up(d)
        w_down(d)
    w_side(0)
    for d in range(1, nz):
        w_up(d)
        w_side(d)
    for d in range(nz):
        kv_side(d)

    scale = 1.0 / math.sqrt(dh)
    lam_init = 0.8 - 0.6 * math.exp(-0.3 * (LAYER - 1))
    lam = [lam_ref[i] for i in range(4)]
    mixing = (
        jnp.exp(jnp.sum(lam[0] * lam[1], -1, keepdims=True))
        - jnp.exp(jnp.sum(lam[2] * lam[3], -1, keepdims=True))
        + lam_init
    )
    blocks_here = tok // BLK

    def score(m):
        q = q_ref[:, m * dh : (m + 1) * dh]
        for b in range(n):
            scores[m, :, b * tok : (b + 1) * tok] = lax.dot_general(
                q, kv[b, 0, :, m * dh : (m + 1) * dh], (((1,), (1,)), ((), ())),
                preferred_element_type=jnp.float32,
            ) * scale

    part = 64

    def soften(i, carry):
        at = pl.multiple_of(i * part, part)
        key_pos = lax.broadcasted_iota(jnp.int32, (1, n * tok), 1)
        key_block = key_pos // BLK
        which = i // (BLK // part)
        block = c * blocks_here + which
        length = len_ref[0]
        stride = [stride_ref[0, j] for j in range(NSTR)]
        for g in range(1, blocks_here):
            length = jnp.where(which == g, len_ref[g], length)
            stride = [jnp.where(which == g, stride_ref[g, j], stride[j]) for j in range(NSTR)]
        floor = block - length
        ok = key_block > floor
        for j in range(NSTR):
            ok = ok | (key_block == stride[j])
        for j in range(GLOB):
            g = glob_ref[j]
            ok = ok | ((key_block == g) & (key_block <= floor))
        last = jnp.where(ok, key_pos, n * tok)
        query = c * tok + at + lax.broadcasted_iota(jnp.int32, (part, 1), 0)
        allowed = last <= query
        maps = []
        for m in range(2):
            s = jnp.where(allowed, scores[m, pl.ds(at, part), :], MASKED)
            e = jnp.exp(s - jnp.max(s, -1, keepdims=True))
            maps.append((e, 1.0 / jnp.sum(e, -1, keepdims=True)))
        (e1, r1), (e2, r2) = maps
        probs[pl.ds(at, part), :] = (e1 * r1 - e2 * (mixing * r2)).astype(probs.dtype)
        return carry

    score(0)
    score(1)
    for d in range(1, nz):
        w_side(-d)
    lax.fori_loop(0, tok // part, soften, 0)
    mixed = jnp.zeros((tok, width), jnp.float32)
    for b in range(n):
        mixed = mixed + jnp.dot(
            probs[:, b * tok : (b + 1) * tok], kv[b, 1], preferred_element_type=jnp.float32
        )
    normed = mixed * lax.rsqrt(jnp.mean(mixed * mixed, -1, keepdims=True) + 1e-05) * (1.0 - lam_init)
    mine[...] = normed.astype(mine.dtype)
    trade = remote(mine, theirs, nm_s, nm_r, core)
    trade.start()

    def twin_at(d, here):
        @pl.when((z + d < nz) & (z + d >= 0))
        def _():
            w_twin(2 * (z + d) + (x if here else 1 - x))

    for d in range(1, nz):
        twin_at(d, True)
    twin_at(0, False)
    for d in range(1, nz):
        twin_at(-d, True)
        twin_at(d, False)
    for d in range(1, nz):
        twin_at(-d, False)
    trade.wait()

    for j in range(nh):
        for which in range(2):
            swap_copy(h * nh + j, which).wait_recv()
        block = None
        for left, weight in ((mine, wown.at[h * nh + j]), (theirs, wother.at[j])):
            piece = lax.dot_general(
                left[...], weight[...], (((1,), (1,)), ((), ())), preferred_element_type=jnp.float32
            ).astype(jnp.bfloat16).astype(jnp.float32)
            block = piece if block is None else block + piece
        obuf[j] = block.astype(obuf.dtype)
        pltpu.make_async_copy(obuf.at[j], out_ref.at[:, pl.ds(j * rows, rows)], out_s.at[j]).start()

    for b in range(n):
        zb, same = b // 2, (b % 2) == x

        @pl.when(same & has_up & (zb <= z))
        def _(b=b):
            kv_copy(b, kvu_s, up).wait_send()
            w_copy(b, wu_s, up).wait_send()

        @pl.when(same & ((zb < z) | ((zb == z) & (x == 0))))
        def _(b=b):
            kv_copy(b, kvx_s, side).wait_send()

        @pl.when(same & has_down & (zb >= z))
        def _(b=b):
            w_copy(b, wd_s, down).wait_send()

        @pl.when(same)
        def _(b=b):
            w_copy(b, wx_s, side).wait_send()

        @pl.when(c != b)
        def _(b=b):
            y_copy(b, lo).wait_send()

    for j in range(nh):
        for which in range(2):
            swap_copy((1 - h) * nh + j, which).wait_send()
        pltpu.make_async_copy(obuf.at[j], out_ref.at[:, pl.ds(j * rows, rows)], out_s.at[j]).wait()


def fused(queries, keys, values, lambda_vectors, out_weight, local_len, stride_keys, global_blocks):
    n = lax.axis_size("ctx")
    tok, _, width = queries.shape
    rows = out_weight.shape[0]
    nh = n // 2
    vmem = pl.BlockSpec(memory_space=pltpu.VMEM)
    smem = pl.BlockSpec(memory_space=pltpu.SMEM)
    hbm = pl.BlockSpec(memory_space=pl.ANY)
    dma = pltpu.SemaphoreType.DMA
    bf16 = jnp.bfloat16
    return pl.pallas_call(
        functools.partial(kernel, n),
        out_shape=jax.ShapeDtypeStruct((tok, nh * rows), bf16),
        in_specs=[vmem, vmem, vmem, hbm, vmem, smem, smem, smem],
        out_specs=hbm,
        scratch_shapes=[
            pltpu.VMEM((n, 2, tok, width), bf16),
            pltpu.VMEM((n, rows, width), bf16),
            pltpu.VMEM((nh, rows, width), bf16),
            pltpu.VMEM((2, tok, n * tok), jnp.float32),
            pltpu.VMEM((tok, n * tok), bf16),
            pltpu.VMEM((tok, width), bf16),
            pltpu.VMEM((tok, width), bf16),
            pltpu.VMEM((nh, tok, rows), bf16),
        ]
        + [dma((n,)) for _ in range(9)]
        + [dma((n,)), dma((n,)), dma, dma, dma, dma((nh,))],
        compiler_params=pltpu.CompilerParams(
            collective_id=0, has_side_effects=True, vmem_limit_bytes=40 * 2**20
        ),
    )(
        queries.reshape(tok, width), keys.reshape(tok, width), values.reshape(tok, width),
        out_weight, lambda_vectors, local_len, stride_keys, global_blocks,
    )


def solution(mesh):
    in_specs = (
        P(("groups", "ctx"), "head", None),
        P(("groups", "ctx"), "head", None),
        P(("groups", "ctx"), "head", None),
        P(None, "head", None),
        P("ctx", "head"),
        P(("groups", "ctx")),
        P(("groups", "ctx"), None),
        P("groups"),
    )
    out_specs = P(("groups", "ctx"), "head")
    shape = mesh.shape

    def layer(queries, *rest):
        per_device = queries.shape[0] // (shape["groups"] * shape["ctx"])
        score_bytes = 8 * per_device * per_device * shape["ctx"]
        fits = score_bytes <= 8 * 2**20 and shape["groups"] == 2 and shape["head"] == 2
        chosen = fused if fits and shape["ctx"] % 2 == 0 else body
        mapped = jax.shard_map(chosen, mesh=mesh, in_specs=in_specs, out_specs=out_specs, check_vma=False)
        return mapped(queries, *rest)

    return layer
```

```python
import functools
import math

import jax
import jax.numpy as jnp
from jax import lax
from jax.experimental import pallas as pl
from jax.experimental.pallas import tpu as pltpu
from jax.sharding import PartitionSpec as P

BLK = 128
NSTR = 3
GLOB = 4
LAYER = 12


def shifted(shard, axis, by):
    length = lax.axis_size(axis)
    pairs = [(i, i + by) for i in range(length) if 0 <= i + by < length]
    return lax.ppermute(shard, axis, pairs)


def from_root(value, axis, source):
    kept = jnp.where(lax.axis_index(axis) == source, value, 0).astype(value.dtype)
    return lax.psum(kept, axis)


def masked_softmax(scores, allowed):
    masked_scores = jnp.where(allowed, scores, -jnp.inf)
    highest = jnp.max(masked_scores, -1, keepdims=True)
    raised = jnp.where(allowed, jnp.exp(masked_scores - highest), 0.0)
    return raised / jnp.sum(raised, -1, keepdims=True)


def body(queries, keys, values, lambda_vectors, out_weight, local_len, stride_keys, global_blocks):
    tok_dev, heads_here, double_width = queries.shape
    head_dim = double_width // 2
    blocks_here = tok_dev // BLK
    ctx_count = lax.axis_size("ctx")
    ctx_pos = lax.axis_index("ctx")
    step_dev = ctx_count // (NSTR + 1)
    lam_init = 0.8 - 0.6 * math.exp(-0.3 * (LAYER - 1))
    mixing = (
        jnp.exp(jnp.sum(lambda_vectors[0] * lambda_vectors[1], -1))
        - jnp.exp(jnp.sum(lambda_vectors[2] * lambda_vectors[3], -1))
        + lam_init
    )
    key_vals = jnp.concatenate((keys, values), axis=-1)
    prev_data = shifted(key_vals, "ctx", 1)
    remote = []
    moving = key_vals
    for slot_pos in range(NSTR):
        moving = shifted(moving, "ctx", step_dev)
        remote.append(moving)
    global_list = []
    for global_pos in range(GLOB):
        block_id = global_blocks[global_pos]
        owner_pos = block_id // blocks_here
        first_row = block_id % blocks_here * BLK
        block_data = lax.dynamic_slice_in_dim(key_vals, first_row, BLK, 0)
        global_list.append(from_root(block_data, "ctx", owner_pos))
    global_data = jnp.concatenate(global_list, 0)
    candidates = jnp.concatenate([key_vals, prev_data] + remote + [global_data], 0)
    cand_keys = candidates[..., :double_width]
    cand_values = candidates[..., double_width:]
    rows_here = jnp.arange(tok_dev, dtype=jnp.int32)
    query_pos = ctx_pos * tok_dev + rows_here
    query_block = query_pos // BLK
    owner_mask = (rows_here // BLK)[:, None] == jnp.arange(blocks_here, dtype=jnp.int32)[None, :]
    length = jnp.sum(jnp.where(owner_mask, local_len[None, :], 0), 1)
    stride_rows = jnp.sum(jnp.where(owner_mask[:, :, None], stride_keys[None, :, :], 0), 1)
    window_floor = query_block - length
    own_block = ctx_pos * blocks_here + rows_here // BLK
    own_ok = (own_block[None, :] > window_floor[:, None]) & (
        query_pos[None, :] - rows_here[:, None] + rows_here[None, :] <= query_pos[:, None]
    )
    prev_block = (ctx_pos - 1) * blocks_here + rows_here // BLK
    prev_ok = (prev_block[None, :] > window_floor[:, None]) & (prev_block[None, :] >= 0)
    masks = [own_ok, prev_ok]
    for slot_pos in range(NSTR):
        far_block = (ctx_pos - (slot_pos + 1) * step_dev) * blocks_here + rows_here // BLK
        listed = stride_rows[:, slot_pos][:, None]
        masks.append((listed == far_block[None, :]) & (listed >= 0))
    in_stride = jnp.any(stride_rows[:, :, None] == global_blocks[None, None, :], 1)
    global_key = jnp.repeat(global_blocks, BLK)
    global_ok = (global_key[None, :] <= window_floor[:, None]) & jnp.logical_not(
        jnp.repeat(in_stride, BLK, axis=1)
    )
    masks.append(global_ok)
    allowed = jnp.concatenate(masks, 1)
    score_scale = 1.0 / math.sqrt(head_dim)
    scores_one = (
        jnp.einsum(
            "qhd,khd->hqk",
            queries[..., :head_dim],
            cand_keys[..., :head_dim],
            preferred_element_type=jnp.float32,
        )
        * score_scale
    )
    scores_two = (
        jnp.einsum(
            "qhd,khd->hqk",
            queries[..., head_dim:],
            cand_keys[..., head_dim:],
            preferred_element_type=jnp.float32,
        )
        * score_scale
    )
    attn_one = masked_softmax(scores_one, allowed)
    attn_two = masked_softmax(scores_two, allowed)
    weights = (attn_one - mixing[:, None, None] * attn_two).astype(jnp.bfloat16)
    mixed_out = jnp.einsum("hqk,khe->qhe", weights, cand_values, preferred_element_type=jnp.float32)
    normed = (
        mixed_out
        * lax.rsqrt(jnp.mean(mixed_out * mixed_out, -1, keepdims=True) + 1e-05)
        * (1.0 - lam_init)
    ).astype(jnp.bfloat16)
    flat_heads = normed.reshape(tok_dev, heads_here * double_width)
    partials = lax.dot_general(
        flat_heads,
        lax.all_gather(out_weight, "ctx", axis=0, tiled=True),
        (((1,), (1,)), ((), ())),
        preferred_element_type=jnp.float32,
    )
    return lax.psum_scatter(partials.astype(jnp.bfloat16), "head", scatter_dimension=1, tiled=True)


MESH_ID = pl.DeviceIdType.MESH
MASKED = -1e30


def kernel(
    n, q_hbm, k_ref, v_ref, w_ref, lam_ref, len_ref, stride_ref, glob_ref, out_ref,
    q_ref, kv, wown, wother, scores, probs, mine, theirs, obuf,
    kvu_s, kvx_s, kv_r, wu_s, wd_s, wx_s, w_r, wy_s, wy_r, sw_s, sw_r, nm_s, nm_r, loc, out_s,
):
    tok, width = q_ref.shape
    dh = width // 2
    rows = w_ref.shape[0]
    half = rows // 2
    nz, nh = n // 2, n // 2
    y, c, h = lax.axis_index("groups"), lax.axis_index("ctx"), lax.axis_index("head")
    z, x = c // 2, c % 2
    has_up, has_down = z + 1 < nz, z >= 1
    up, down, side = {"ctx": c + 2}, {"ctx": c - 2}, {"ctx": c + 1 - 2 * x}
    twin, core = {"groups": 1 - y}, {"head": 1 - h}
    lo = pl.multiple_of(y * half, half)
    hi = pl.multiple_of((1 - y) * half, half)

    barrier = pltpu.get_barrier_semaphore()
    for to in (side, twin, core):
        pl.semaphore_signal(barrier, inc=1, device_id=to, device_id_type=MESH_ID)

    @pl.when(has_up)
    def _():
        pl.semaphore_signal(barrier, inc=1, device_id=up, device_id_type=MESH_ID)

    @pl.when(has_down)
    def _():
        pl.semaphore_signal(barrier, inc=1, device_id=down, device_id_type=MESH_ID)

    loads = [
        pltpu.make_async_copy(src, dst, loc.at[i])
        for i, (src, dst) in enumerate(
            ((k_ref, kv.at[c, 0]), (v_ref, kv.at[c, 1]), (w_ref, wown.at[c]), (q_hbm, q_ref))
        )
    ]
    for load in loads:
        load.start()
    pl.semaphore_wait(barrier, 3 + has_up.astype(jnp.int32) + has_down.astype(jnp.int32))

    def remote(src, dst, send, recv, to):
        return pltpu.make_async_remote_copy(
            src_ref=src, dst_ref=dst, send_sem=send, recv_sem=recv, device_id=to, device_id_type=MESH_ID
        )

    def kv_copy(b, send, to):
        return remote(kv.at[b], kv.at[b], send.at[b], kv_r.at[b], to)

    def w_copy(b, send, to):
        piece = wown.at[b, pl.ds(lo, half)]
        return remote(piece, piece, send.at[b], w_r.at[b], to)

    def y_copy(b, start):
        piece = wown.at[b, pl.ds(start, half)]
        return remote(piece, piece, wy_s.at[b], wy_r.at[b], twin)

    def swap_copy(b, which):
        start = pl.multiple_of(which * half, half)
        slot = b % nh
        return remote(
            wown.at[b, pl.ds(start, half)], wother.at[slot, pl.ds(start, half)],
            sw_s.at[2 * slot + which], sw_r.at[2 * slot + which], core,
        )

    def swap(b, which):
        @pl.when(b // nh == 1 - h)
        def _():
            swap_copy(b, which).start()

    def kv_up(d):
        @pl.when(z >= d)
        def _():
            b = c - 2 * d
            kv_copy(b, kvu_s, up).wait_recv()

            @pl.when(has_up)
            def _():
                kv_copy(b, kvu_s, up).start()

            kv_copy(b, kvx_s, side).start()

    def w_down(d):
        @pl.when(z + d < nz)
        def _():
            b = c + 2 * d
            w_copy(b, wd_s, down).wait_recv()

            @pl.when(has_down)
            def _():
                w_copy(b, wd_s, down).start()

            y_copy(b, lo).start()
            w_copy(b, wx_s, side).start()
            swap(b, y)

    def w_up(d):
        @pl.when(z >= d)
        def _():
            b = c - 2 * d
            w_copy(b, wu_s, up).wait_recv()

            @pl.when(has_up)
            def _():
                w_copy(b, wu_s, up).start()

            y_copy(b, lo).start()
            w_copy(b, wx_s, side).start()
            swap(b, y)

    def w_side(d):
        @pl.when((z + d < nz) & (z + d >= 0))
        def _():
            b = 2 * (z + d) + 1 - x
            w_copy(b, wx_s, side).wait_recv()
            y_copy(b, lo).start()
            swap(b, y)

    def w_twin(b):
        y_copy(b, hi).wait_recv()
        swap(b, 1 - y)

    def kv_side(d):
        @pl.when((z >= d) & ((d > 0) | (x == 1)))
        def _():
            b = 2 * (z - d) + 1 - x
            kv_copy(b, kvx_s, side).wait_recv()

    loads[0].wait()
    loads[1].wait()

    @pl.when(has_up)
    def _():
        kv_copy(c, kvu_s, up).start()

    @pl.when(x == 0)
    def _():
        kv_copy(c, kvx_s, side).start()

    loads[2].wait()

    @pl.when(has_down)
    def _():
        w_copy(c, wd_s, down).start()

    w_copy(c, wx_s, side).start()

    @pl.when(has_up)
    def _():
        w_copy(c, wu_s, up).start()

    swap(c, 0)
    swap(c, 1)

    for b in range(1, n):
        @pl.when(c < b)
        def _(b=b):
            kv[b] = jnp.zeros(kv.shape[1:], kv.dtype)

    for d in range(1, nz):
        kv_up(d)
        w_down(d)
    scale = 1.0 / math.sqrt(dh)
    lam_init = 0.8 - 0.6 * math.exp(-0.3 * (LAYER - 1))
    lam = [lam_ref[i] for i in range(4)]
    mixing = (
        jnp.exp(jnp.sum(lam[0] * lam[1], -1, keepdims=True))
        - jnp.exp(jnp.sum(lam[2] * lam[3], -1, keepdims=True))
        + lam_init
    )
    blocks_here = tok // BLK

    def score(m):
        q = q_ref[:, m * dh : (m + 1) * dh]
        for b in range(n):
            scores[m, :, b * tok : (b + 1) * tok] = lax.dot_general(
                q, kv[b, 0, :, m * dh : (m + 1) * dh], (((1,), (1,)), ((), ())),
                preferred_element_type=jnp.float32,
            ) * scale

    part = 64

    def soften(i, carry):
        at = pl.multiple_of(i * part, part)
        key_pos = lax.broadcasted_iota(jnp.int32, (1, n * tok), 1)
        key_block = key_pos // BLK
        which = i // (BLK // part)
        block = c * blocks_here + which
        length = len_ref[0]
        stride = [stride_ref[0, j] for j in range(NSTR)]
        for g in range(1, blocks_here):
            length = jnp.where(which == g, len_ref[g], length)
            stride = [jnp.where(which == g, stride_ref[g, j], stride[j]) for j in range(NSTR)]
        floor = block - length
        ok = key_block > floor
        for j in range(NSTR):
            ok = ok | (key_block == stride[j])
        for j in range(GLOB):
            g = glob_ref[j]
            ok = ok | ((key_block == g) & (key_block <= floor))
        last = jnp.where(ok, key_pos, n * tok)
        query = c * tok + at + lax.broadcasted_iota(jnp.int32, (part, 1), 0)
        allowed = last <= query
        maps = []
        for m in range(2):
            s = jnp.where(allowed, scores[m, pl.ds(at, part), :], MASKED)
            e = jnp.exp(s - jnp.max(s, -1, keepdims=True))
            maps.append((e, 1.0 / jnp.sum(e, -1, keepdims=True)))
        (e1, r1), (e2, r2) = maps
        probs[pl.ds(at, part), :] = (e1 * r1 - e2 * (mixing * r2)).astype(probs.dtype)
        return carry

    chunks = tok // part
    done = 0
    w_side(0)
    for d in range(1, nz + 1):
        if d < nz:
            w_up(d)
            w_side(d)
        if d > 1:
            w_side(1 - d)
        if d == max(nz - 2, 1):
            for far in range(nz):
                kv_side(far)
            loads[3].wait()
            score(0)
            score(1)
        if d >= max(nz - 2, 1) and done < chunks:
            soften(done, 0)
            done += 1
    for i in range(done, chunks):
        soften(i, 0)
    mixed = jnp.zeros((tok, width), jnp.float32)
    for b in range(n):
        mixed = mixed + jnp.dot(
            probs[:, b * tok : (b + 1) * tok], kv[b, 1], preferred_element_type=jnp.float32
        )
    normed = mixed * lax.rsqrt(jnp.mean(mixed * mixed, -1, keepdims=True) + 1e-05) * (1.0 - lam_init)
    mine[...] = normed.astype(mine.dtype)
    trade = remote(mine, theirs, nm_s, nm_r, core)
    trade.start()

    def twin_at(d, here):
        @pl.when((z + d < nz) & (z + d >= 0))
        def _():
            w_twin(2 * (z + d) + (x if here else 1 - x))

    for d in range(1, nz):
        twin_at(d, True)
    twin_at(0, False)
    for d in range(1, nz):
        twin_at(-d, True)
        twin_at(d, False)
    for d in range(1, nz):
        twin_at(-d, False)
    trade.wait()

    for i in range(nh):
        j = jnp.where(z >= nz // 2, nh - 1 - i, i)
        for which in range(2):
            swap_copy(h * nh + j, which).wait_recv()
        block = None
        for left, weight in ((mine, wown.at[h * nh + j]), (theirs, wother.at[j])):
            piece = lax.dot_general(
                left[...], weight[...], (((1,), (1,)), ((), ())), preferred_element_type=jnp.float32
            ).astype(jnp.bfloat16).astype(jnp.float32)
            block = piece if block is None else block + piece
        obuf[i] = block.astype(obuf.dtype)
        at = pl.multiple_of(j * rows, rows)
        pltpu.make_async_copy(obuf.at[i], out_ref.at[:, pl.ds(at, rows)], out_s.at[i]).start()

    for b in range(n):
        zb, same = b // 2, (b % 2) == x

        @pl.when(same & has_up & (zb <= z))
        def _(b=b):
            kv_copy(b, kvu_s, up).wait_send()
            w_copy(b, wu_s, up).wait_send()

        @pl.when(same & ((zb < z) | ((zb == z) & (x == 0))))
        def _(b=b):
            kv_copy(b, kvx_s, side).wait_send()

        @pl.when(same & has_down & (zb >= z))
        def _(b=b):
            w_copy(b, wd_s, down).wait_send()

        @pl.when(same)
        def _(b=b):
            w_copy(b, wx_s, side).wait_send()

        @pl.when(c != b)
        def _(b=b):
            y_copy(b, lo).wait_send()

    for j in range(nh):
        for which in range(2):
            swap_copy((1 - h) * nh + j, which).wait_send()
        pltpu.make_async_copy(obuf.at[j], out_ref.at[:, pl.ds(j * rows, rows)], out_s.at[j]).wait()


def fused(queries, keys, values, lambda_vectors, out_weight, local_len, stride_keys, global_blocks):
    n = lax.axis_size("ctx")
    tok, _, width = queries.shape
    rows = out_weight.shape[0]
    nh = n // 2
    vmem = pl.BlockSpec(memory_space=pltpu.VMEM)
    smem = pl.BlockSpec(memory_space=pltpu.SMEM)
    hbm = pl.BlockSpec(memory_space=pl.ANY)
    dma = pltpu.SemaphoreType.DMA
    bf16 = jnp.bfloat16
    return pl.pallas_call(
        functools.partial(kernel, n),
        out_shape=jax.ShapeDtypeStruct((tok, nh * rows), bf16),
        in_specs=[hbm, hbm, hbm, hbm, vmem, smem, smem, smem],
        out_specs=hbm,
        scratch_shapes=[
            pltpu.VMEM((tok, width), bf16),
            pltpu.VMEM((n, 2, tok, width), bf16),
            pltpu.VMEM((n, rows, width), bf16),
            pltpu.VMEM((nh, rows, width), bf16),
            pltpu.VMEM((2, tok, n * tok), jnp.float32),
            pltpu.VMEM((tok, n * tok), bf16),
            pltpu.VMEM((tok, width), bf16),
            pltpu.VMEM((tok, width), bf16),
            pltpu.VMEM((nh, tok, rows), bf16),
        ]
        + [dma((n,)) for _ in range(9)]
        + [dma((n,)), dma((n,)), dma, dma, dma((4,)), dma((nh,))],
        compiler_params=pltpu.CompilerParams(
            collective_id=0, has_side_effects=True, vmem_limit_bytes=60 * 2**20
        ),
    )(
        queries.reshape(tok, width), keys.reshape(tok, width), values.reshape(tok, width),
        out_weight, lambda_vectors, local_len, stride_keys, global_blocks,
    )


def solution(mesh):
    in_specs = (
        P(("groups", "ctx"), "head", None),
        P(("groups", "ctx"), "head", None),
        P(("groups", "ctx"), "head", None),
        P(None, "head", None),
        P("ctx", "head"),
        P(("groups", "ctx")),
        P(("groups", "ctx"), None),
        P("groups"),
    )
    out_specs = P(("groups", "ctx"), "head")
    shape = mesh.shape

    def layer(queries, *rest):
        per_device = queries.shape[0] // (shape["groups"] * shape["ctx"])
        score_bytes = 8 * per_device * per_device * shape["ctx"]
        fits = score_bytes <= 8 * 2**20 and shape["groups"] == 2 and shape["head"] == 2
        chosen = fused if fits and shape["ctx"] % 2 == 0 else body
        mapped = jax.shard_map(chosen, mesh=mesh, in_specs=in_specs, out_specs=out_specs, check_vma=False)
        return mapped(queries, *rest)

    return layer
```

```python
import functools
import math

import jax
import jax.numpy as jnp
from jax import lax
from jax.experimental import pallas as pl
from jax.experimental.pallas import tpu as pltpu
from jax.sharding import PartitionSpec as P

BLK = 128
NSTR = 3
GLOB = 4
LAYER = 12


def shifted(shard, axis, by):
    length = lax.axis_size(axis)
    pairs = [(i, i + by) for i in range(length) if 0 <= i + by < length]
    return lax.ppermute(shard, axis, pairs)


def from_root(value, axis, source):
    kept = jnp.where(lax.axis_index(axis) == source, value, 0).astype(value.dtype)
    return lax.psum(kept, axis)


def masked_softmax(scores, allowed):
    masked_scores = jnp.where(allowed, scores, -jnp.inf)
    highest = jnp.max(masked_scores, -1, keepdims=True)
    raised = jnp.where(allowed, jnp.exp(masked_scores - highest), 0.0)
    return raised / jnp.sum(raised, -1, keepdims=True)


def body(queries, keys, values, lambda_vectors, out_weight, local_len, stride_keys, global_blocks):
    tok_dev, heads_here, double_width = queries.shape
    head_dim = double_width // 2
    blocks_here = tok_dev // BLK
    ctx_count = lax.axis_size("ctx")
    ctx_pos = lax.axis_index("ctx")
    step_dev = ctx_count // (NSTR + 1)
    lam_init = 0.8 - 0.6 * math.exp(-0.3 * (LAYER - 1))
    mixing = (
        jnp.exp(jnp.sum(lambda_vectors[0] * lambda_vectors[1], -1))
        - jnp.exp(jnp.sum(lambda_vectors[2] * lambda_vectors[3], -1))
        + lam_init
    )
    key_vals = jnp.concatenate((keys, values), axis=-1)
    prev_data = shifted(key_vals, "ctx", 1)
    remote = []
    moving = key_vals
    for slot_pos in range(NSTR):
        moving = shifted(moving, "ctx", step_dev)
        remote.append(moving)
    global_list = []
    for global_pos in range(GLOB):
        block_id = global_blocks[global_pos]
        owner_pos = block_id // blocks_here
        first_row = block_id % blocks_here * BLK
        block_data = lax.dynamic_slice_in_dim(key_vals, first_row, BLK, 0)
        global_list.append(from_root(block_data, "ctx", owner_pos))
    global_data = jnp.concatenate(global_list, 0)
    candidates = jnp.concatenate([key_vals, prev_data] + remote + [global_data], 0)
    cand_keys = candidates[..., :double_width]
    cand_values = candidates[..., double_width:]
    rows_here = jnp.arange(tok_dev, dtype=jnp.int32)
    query_pos = ctx_pos * tok_dev + rows_here
    query_block = query_pos // BLK
    owner_mask = (rows_here // BLK)[:, None] == jnp.arange(blocks_here, dtype=jnp.int32)[None, :]
    length = jnp.sum(jnp.where(owner_mask, local_len[None, :], 0), 1)
    stride_rows = jnp.sum(jnp.where(owner_mask[:, :, None], stride_keys[None, :, :], 0), 1)
    window_floor = query_block - length
    own_block = ctx_pos * blocks_here + rows_here // BLK
    own_ok = (own_block[None, :] > window_floor[:, None]) & (
        query_pos[None, :] - rows_here[:, None] + rows_here[None, :] <= query_pos[:, None]
    )
    prev_block = (ctx_pos - 1) * blocks_here + rows_here // BLK
    prev_ok = (prev_block[None, :] > window_floor[:, None]) & (prev_block[None, :] >= 0)
    masks = [own_ok, prev_ok]
    for slot_pos in range(NSTR):
        far_block = (ctx_pos - (slot_pos + 1) * step_dev) * blocks_here + rows_here // BLK
        listed = stride_rows[:, slot_pos][:, None]
        masks.append((listed == far_block[None, :]) & (listed >= 0))
    in_stride = jnp.any(stride_rows[:, :, None] == global_blocks[None, None, :], 1)
    global_key = jnp.repeat(global_blocks, BLK)
    global_ok = (global_key[None, :] <= window_floor[:, None]) & jnp.logical_not(
        jnp.repeat(in_stride, BLK, axis=1)
    )
    masks.append(global_ok)
    allowed = jnp.concatenate(masks, 1)
    score_scale = 1.0 / math.sqrt(head_dim)
    scores_one = (
        jnp.einsum(
            "qhd,khd->hqk",
            queries[..., :head_dim],
            cand_keys[..., :head_dim],
            preferred_element_type=jnp.float32,
        )
        * score_scale
    )
    scores_two = (
        jnp.einsum(
            "qhd,khd->hqk",
            queries[..., head_dim:],
            cand_keys[..., head_dim:],
            preferred_element_type=jnp.float32,
        )
        * score_scale
    )
    attn_one = masked_softmax(scores_one, allowed)
    attn_two = masked_softmax(scores_two, allowed)
    weights = (attn_one - mixing[:, None, None] * attn_two).astype(jnp.bfloat16)
    mixed_out = jnp.einsum("hqk,khe->qhe", weights, cand_values, preferred_element_type=jnp.float32)
    normed = (
        mixed_out
        * lax.rsqrt(jnp.mean(mixed_out * mixed_out, -1, keepdims=True) + 1e-05)
        * (1.0 - lam_init)
    ).astype(jnp.bfloat16)
    flat_heads = normed.reshape(tok_dev, heads_here * double_width)
    partials = lax.dot_general(
        flat_heads,
        lax.all_gather(out_weight, "ctx", axis=0, tiled=True),
        (((1,), (1,)), ((), ())),
        preferred_element_type=jnp.float32,
    )
    return lax.psum_scatter(partials.astype(jnp.bfloat16), "head", scatter_dimension=1, tiled=True)


MESH_ID = pl.DeviceIdType.MESH
MASKED = -1e30


def kernel(
    n, q_hbm, k_ref, v_ref, w_ref, lam_ref, len_ref, stride_ref, glob_ref, out_ref,
    q_ref, kv, wown, wother, scores, probs, mine, theirs, obuf,
    kvu_s, kvx_s, kv_r, wu_s, wd_s, wx_s, w_r, wy_s, wy_r, sw_s, sw_r, nm_s, nm_r, loc, out_s,
):
    tok, width = q_ref.shape
    dh = width // 2
    rows = w_ref.shape[0]
    half = rows // 2
    nz, nh = n // 2, n // 2
    y, c, h = lax.axis_index("groups"), lax.axis_index("ctx"), lax.axis_index("head")
    z, x = c // 2, c % 2
    has_up, has_down = z + 1 < nz, z >= 1
    up, down, side = {"ctx": c + 2}, {"ctx": c - 2}, {"ctx": c + 1 - 2 * x}
    twin, core = {"groups": 1 - y}, {"head": 1 - h}
    lo = pl.multiple_of(y * half, half)
    hi = pl.multiple_of((1 - y) * half, half)

    barrier = pltpu.get_barrier_semaphore()
    for to in (side, twin, core):
        pl.semaphore_signal(barrier, inc=1, device_id=to, device_id_type=MESH_ID)

    @pl.when(has_up)
    def _():
        pl.semaphore_signal(barrier, inc=1, device_id=up, device_id_type=MESH_ID)

    @pl.when(has_down)
    def _():
        pl.semaphore_signal(barrier, inc=1, device_id=down, device_id_type=MESH_ID)

    loads = [
        pltpu.make_async_copy(src, dst, loc.at[i])
        for i, (src, dst) in enumerate(
            ((k_ref, kv.at[c, 0]), (v_ref, kv.at[c, 1]), (w_ref, wown.at[c]), (q_hbm, q_ref))
        )
    ]
    for load in loads:
        load.start()
    pl.semaphore_wait(barrier, 3 + has_up.astype(jnp.int32) + has_down.astype(jnp.int32))

    def remote(src, dst, send, recv, to):
        return pltpu.make_async_remote_copy(
            src_ref=src, dst_ref=dst, send_sem=send, recv_sem=recv, device_id=to, device_id_type=MESH_ID
        )

    def kv_copy(b, send, to):
        return remote(kv.at[b], kv.at[b], send.at[b], kv_r.at[b], to)

    def w_copy(b, send, to):
        piece = wown.at[b, pl.ds(lo, half)]
        return remote(piece, piece, send.at[b], w_r.at[b], to)

    def y_copy(b, start):
        piece = wown.at[b, pl.ds(start, half)]
        return remote(piece, piece, wy_s.at[b], wy_r.at[b], twin)

    def swap_copy(b, which):
        start = pl.multiple_of(which * half, half)
        slot = b % nh
        return remote(
            wown.at[b, pl.ds(start, half)], wother.at[slot, pl.ds(start, half)],
            sw_s.at[2 * slot + which], sw_r.at[2 * slot + which], core,
        )

    def swap(b, which):
        @pl.when(b // nh == 1 - h)
        def _():
            swap_copy(b, which).start()

    def kv_up(d):
        @pl.when(z >= d)
        def _():
            b = c - 2 * d
            kv_copy(b, kvu_s, up).wait_recv()

            @pl.when(has_up)
            def _():
                kv_copy(b, kvu_s, up).start()

            kv_copy(b, kvx_s, side).start()

    def w_down(d):
        @pl.when(z + d < nz)
        def _():
            b = c + 2 * d
            w_copy(b, wd_s, down).wait_recv()

            @pl.when(has_down)
            def _():
                w_copy(b, wd_s, down).start()

            y_copy(b, lo).start()
            w_copy(b, wx_s, side).start()
            swap(b, y)

    def w_up(d):
        @pl.when(z >= d)
        def _():
            b = c - 2 * d
            w_copy(b, wu_s, up).wait_recv()

            @pl.when(has_up)
            def _():
                w_copy(b, wu_s, up).start()

            y_copy(b, lo).start()
            w_copy(b, wx_s, side).start()
            swap(b, y)

    def w_side(d):
        @pl.when((z + d < nz) & (z + d >= 0))
        def _():
            b = 2 * (z + d) + 1 - x
            w_copy(b, wx_s, side).wait_recv()
            y_copy(b, lo).start()
            swap(b, y)

    def w_twin(b):
        y_copy(b, hi).wait_recv()
        swap(b, 1 - y)

    def kv_side(d):
        @pl.when((z >= d) & ((d > 0) | (x == 1)))
        def _():
            b = 2 * (z - d) + 1 - x
            kv_copy(b, kvx_s, side).wait_recv()

    loads[0].wait()
    loads[1].wait()

    @pl.when(has_up)
    def _():
        kv_copy(c, kvu_s, up).start()

    @pl.when(x == 0)
    def _():
        kv_copy(c, kvx_s, side).start()

    loads[2].wait()

    @pl.when(has_down)
    def _():
        w_copy(c, wd_s, down).start()

    w_copy(c, wx_s, side).start()

    @pl.when(has_up)
    def _():
        w_copy(c, wu_s, up).start()

    swap(c, 0)
    swap(c, 1)

    for b in range(1, n):
        @pl.when(c < b)
        def _(b=b):
            kv[b] = jnp.zeros(kv.shape[1:], kv.dtype)

    for d in range(1, nz):
        kv_up(d)
        w_down(d)
        w_up(d)
        w_side(d - 1)
        if d > 1:
            w_side(1 - d)

    scale = 1.0 / math.sqrt(dh)
    lam_init = 0.8 - 0.6 * math.exp(-0.3 * (LAYER - 1))
    lam = [lam_ref[i] for i in range(4)]
    mixing = (
        jnp.exp(jnp.sum(lam[0] * lam[1], -1, keepdims=True))
        - jnp.exp(jnp.sum(lam[2] * lam[3], -1, keepdims=True))
        + lam_init
    )
    blocks_here = tok // BLK

    def score(m):
        q = q_ref[:, m * dh : (m + 1) * dh]
        for b in range(n):
            scores[m, :, b * tok : (b + 1) * tok] = lax.dot_general(
                q, kv[b, 0, :, m * dh : (m + 1) * dh], (((1,), (1,)), ((), ())),
                preferred_element_type=jnp.float32,
            ) * scale

    part = 64

    def soften(i, carry):
        at = pl.multiple_of(i * part, part)
        key_pos = lax.broadcasted_iota(jnp.int32, (1, n * tok), 1)
        key_block = key_pos // BLK
        which = i // (BLK // part)
        block = c * blocks_here + which
        length = len_ref[0]
        stride = [stride_ref[0, j] for j in range(NSTR)]
        for g in range(1, blocks_here):
            length = jnp.where(which == g, len_ref[g], length)
            stride = [jnp.where(which == g, stride_ref[g, j], stride[j]) for j in range(NSTR)]
        floor = block - length
        ok = key_block > floor
        for j in range(NSTR):
            ok = ok | (key_block == stride[j])
        for j in range(GLOB):
            g = glob_ref[j]
            ok = ok | ((key_block == g) & (key_block <= floor))
        last = jnp.where(ok, key_pos, n * tok)
        query = c * tok + at + lax.broadcasted_iota(jnp.int32, (part, 1), 0)
        allowed = last <= query
        maps = []
        for m in range(2):
            s = jnp.where(allowed, scores[m, pl.ds(at, part), :], MASKED)
            e = jnp.exp(s - jnp.max(s, -1, keepdims=True))
            maps.append((e, 1.0 / jnp.sum(e, -1, keepdims=True)))
        (e1, r1), (e2, r2) = maps
        probs[pl.ds(at, part), :] = (e1 * r1 - e2 * (mixing * r2)).astype(probs.dtype)
        return carry

    chunks = tok // part
    w_side(nz - 1)
    for far in range(nz):
        kv_side(far)
    loads[3].wait()
    score(0)
    score(1)
    for i in range(chunks):
        soften(i, 0)
        if i == chunks // 2 - 1:
            w_side(1 - nz)
    mixed = jnp.zeros((tok, width), jnp.float32)
    for b in range(n):
        mixed = mixed + jnp.dot(
            probs[:, b * tok : (b + 1) * tok], kv[b, 1], preferred_element_type=jnp.float32
        )
    normed = mixed * lax.rsqrt(jnp.mean(mixed * mixed, -1, keepdims=True) + 1e-05) * (1.0 - lam_init)
    mine[...] = normed.astype(mine.dtype)
    trade = remote(mine, theirs, nm_s, nm_r, core)
    trade.start()

    def twin_at(d, here):
        @pl.when((z + d < nz) & (z + d >= 0))
        def _():
            w_twin(2 * (z + d) + (x if here else 1 - x))

    for d in range(1, nz):
        twin_at(d, True)
        twin_at(-d, True)
        twin_at(d - 1, False)
        if d > 1:
            twin_at(1 - d, False)
    twin_at(nz - 1, False)
    twin_at(1 - nz, False)
    trade.wait()

    for i in range(nh):
        j = jnp.where(z >= nz // 2, nh - 1 - i, i)
        for which in range(2):
            swap_copy(h * nh + j, which).wait_recv()
        block = None
        for left, weight in ((mine, wown.at[h * nh + j]), (theirs, wother.at[j])):
            piece = lax.dot_general(
                left[...], weight[...], (((1,), (1,)), ((), ())), preferred_element_type=jnp.float32
            ).astype(jnp.bfloat16).astype(jnp.float32)
            block = piece if block is None else block + piece
        obuf[i] = block.astype(obuf.dtype)
        at = pl.multiple_of(j * rows, rows)
        pltpu.make_async_copy(obuf.at[i], out_ref.at[:, pl.ds(at, rows)], out_s.at[i]).start()

    for b in range(n):
        zb, same = b // 2, (b % 2) == x

        @pl.when(same & has_up & (zb <= z))
        def _(b=b):
            kv_copy(b, kvu_s, up).wait_send()
            w_copy(b, wu_s, up).wait_send()

        @pl.when(same & ((zb < z) | ((zb == z) & (x == 0))))
        def _(b=b):
            kv_copy(b, kvx_s, side).wait_send()

        @pl.when(same & has_down & (zb >= z))
        def _(b=b):
            w_copy(b, wd_s, down).wait_send()

        @pl.when(same)
        def _(b=b):
            w_copy(b, wx_s, side).wait_send()

        @pl.when(c != b)
        def _(b=b):
            y_copy(b, lo).wait_send()

    for j in range(nh):
        for which in range(2):
            swap_copy((1 - h) * nh + j, which).wait_send()
        pltpu.make_async_copy(obuf.at[j], out_ref.at[:, pl.ds(j * rows, rows)], out_s.at[j]).wait()


def fused(queries, keys, values, lambda_vectors, out_weight, local_len, stride_keys, global_blocks):
    n = lax.axis_size("ctx")
    tok, _, width = queries.shape
    rows = out_weight.shape[0]
    nh = n // 2
    vmem = pl.BlockSpec(memory_space=pltpu.VMEM)
    smem = pl.BlockSpec(memory_space=pltpu.SMEM)
    hbm = pl.BlockSpec(memory_space=pl.ANY)
    dma = pltpu.SemaphoreType.DMA
    bf16 = jnp.bfloat16
    return pl.pallas_call(
        functools.partial(kernel, n),
        out_shape=jax.ShapeDtypeStruct((tok, nh * rows), bf16),
        in_specs=[hbm, hbm, hbm, hbm, vmem, smem, smem, smem],
        out_specs=hbm,
        scratch_shapes=[
            pltpu.VMEM((tok, width), bf16),
            pltpu.VMEM((n, 2, tok, width), bf16),
            pltpu.VMEM((n, rows, width), bf16),
            pltpu.VMEM((nh, rows, width), bf16),
            pltpu.VMEM((2, tok, n * tok), jnp.float32),
            pltpu.VMEM((tok, n * tok), bf16),
            pltpu.VMEM((tok, width), bf16),
            pltpu.VMEM((tok, width), bf16),
            pltpu.VMEM((nh, tok, rows), bf16),
        ]
        + [dma((n,)) for _ in range(9)]
        + [dma((n,)), dma((n,)), dma, dma, dma((4,)), dma((nh,))],
        compiler_params=pltpu.CompilerParams(
            collective_id=0, has_side_effects=True, vmem_limit_bytes=60 * 2**20
        ),
    )(
        queries.reshape(tok, width), keys.reshape(tok, width), values.reshape(tok, width),
        out_weight, lambda_vectors, local_len, stride_keys, global_blocks,
    )


def solution(mesh):
    in_specs = (
        P(("groups", "ctx"), "head", None),
        P(("groups", "ctx"), "head", None),
        P(("groups", "ctx"), "head", None),
        P(None, "head", None),
        P("ctx", "head"),
        P(("groups", "ctx")),
        P(("groups", "ctx"), None),
        P("groups"),
    )
    out_specs = P(("groups", "ctx"), "head")
    shape = mesh.shape

    def layer(queries, *rest):
        per_device = queries.shape[0] // (shape["groups"] * shape["ctx"])
        score_bytes = 8 * per_device * per_device * shape["ctx"]
        fits = score_bytes <= 8 * 2**20 and shape["groups"] == 2 and shape["head"] == 2
        chosen = fused if fits and shape["ctx"] % 2 == 0 else body
        mapped = jax.shard_map(chosen, mesh=mesh, in_specs=in_specs, out_specs=out_specs, check_vma=False)
        return mapped(queries, *rest)

    return layer
```

```python
import functools
import math

import jax
import jax.numpy as jnp
from jax import lax
from jax.experimental import pallas as pl
from jax.experimental.pallas import tpu as pltpu
from jax.sharding import PartitionSpec as P

BLK = 128
NSTR = 3
GLOB = 4
LAYER = 12


def shifted(shard, axis, by):
    length = lax.axis_size(axis)
    pairs = [(i, i + by) for i in range(length) if 0 <= i + by < length]
    return lax.ppermute(shard, axis, pairs)


def from_root(value, axis, source):
    kept = jnp.where(lax.axis_index(axis) == source, value, 0).astype(value.dtype)
    return lax.psum(kept, axis)


def masked_softmax(scores, allowed):
    masked_scores = jnp.where(allowed, scores, -jnp.inf)
    highest = jnp.max(masked_scores, -1, keepdims=True)
    raised = jnp.where(allowed, jnp.exp(masked_scores - highest), 0.0)
    return raised / jnp.sum(raised, -1, keepdims=True)


def body(queries, keys, values, lambda_vectors, out_weight, local_len, stride_keys, global_blocks):
    tok_dev, heads_here, double_width = queries.shape
    head_dim = double_width // 2
    blocks_here = tok_dev // BLK
    ctx_count = lax.axis_size("ctx")
    ctx_pos = lax.axis_index("ctx")
    step_dev = ctx_count // (NSTR + 1)
    lam_init = 0.8 - 0.6 * math.exp(-0.3 * (LAYER - 1))
    mixing = (
        jnp.exp(jnp.sum(lambda_vectors[0] * lambda_vectors[1], -1))
        - jnp.exp(jnp.sum(lambda_vectors[2] * lambda_vectors[3], -1))
        + lam_init
    )
    key_vals = jnp.concatenate((keys, values), axis=-1)
    prev_data = shifted(key_vals, "ctx", 1)
    remote = []
    moving = key_vals
    for slot_pos in range(NSTR):
        moving = shifted(moving, "ctx", step_dev)
        remote.append(moving)
    global_list = []
    for global_pos in range(GLOB):
        block_id = global_blocks[global_pos]
        owner_pos = block_id // blocks_here
        first_row = block_id % blocks_here * BLK
        block_data = lax.dynamic_slice_in_dim(key_vals, first_row, BLK, 0)
        global_list.append(from_root(block_data, "ctx", owner_pos))
    global_data = jnp.concatenate(global_list, 0)
    candidates = jnp.concatenate([key_vals, prev_data] + remote + [global_data], 0)
    cand_keys = candidates[..., :double_width]
    cand_values = candidates[..., double_width:]
    rows_here = jnp.arange(tok_dev, dtype=jnp.int32)
    query_pos = ctx_pos * tok_dev + rows_here
    query_block = query_pos // BLK
    owner_mask = (rows_here // BLK)[:, None] == jnp.arange(blocks_here, dtype=jnp.int32)[None, :]
    length = jnp.sum(jnp.where(owner_mask, local_len[None, :], 0), 1)
    stride_rows = jnp.sum(jnp.where(owner_mask[:, :, None], stride_keys[None, :, :], 0), 1)
    window_floor = query_block - length
    own_block = ctx_pos * blocks_here + rows_here // BLK
    own_ok = (own_block[None, :] > window_floor[:, None]) & (
        query_pos[None, :] - rows_here[:, None] + rows_here[None, :] <= query_pos[:, None]
    )
    prev_block = (ctx_pos - 1) * blocks_here + rows_here // BLK
    prev_ok = (prev_block[None, :] > window_floor[:, None]) & (prev_block[None, :] >= 0)
    masks = [own_ok, prev_ok]
    for slot_pos in range(NSTR):
        far_block = (ctx_pos - (slot_pos + 1) * step_dev) * blocks_here + rows_here // BLK
        listed = stride_rows[:, slot_pos][:, None]
        masks.append((listed == far_block[None, :]) & (listed >= 0))
    in_stride = jnp.any(stride_rows[:, :, None] == global_blocks[None, None, :], 1)
    global_key = jnp.repeat(global_blocks, BLK)
    global_ok = (global_key[None, :] <= window_floor[:, None]) & jnp.logical_not(
        jnp.repeat(in_stride, BLK, axis=1)
    )
    masks.append(global_ok)
    allowed = jnp.concatenate(masks, 1)
    score_scale = 1.0 / math.sqrt(head_dim)
    scores_one = (
        jnp.einsum(
            "qhd,khd->hqk",
            queries[..., :head_dim],
            cand_keys[..., :head_dim],
            preferred_element_type=jnp.float32,
        )
        * score_scale
    )
    scores_two = (
        jnp.einsum(
            "qhd,khd->hqk",
            queries[..., head_dim:],
            cand_keys[..., head_dim:],
            preferred_element_type=jnp.float32,
        )
        * score_scale
    )
    attn_one = masked_softmax(scores_one, allowed)
    attn_two = masked_softmax(scores_two, allowed)
    weights = (attn_one - mixing[:, None, None] * attn_two).astype(jnp.bfloat16)
    mixed_out = jnp.einsum("hqk,khe->qhe", weights, cand_values, preferred_element_type=jnp.float32)
    normed = (
        mixed_out
        * lax.rsqrt(jnp.mean(mixed_out * mixed_out, -1, keepdims=True) + 1e-05)
        * (1.0 - lam_init)
    ).astype(jnp.bfloat16)
    flat_heads = normed.reshape(tok_dev, heads_here * double_width)
    partials = lax.dot_general(
        flat_heads,
        lax.all_gather(out_weight, "ctx", axis=0, tiled=True),
        (((1,), (1,)), ((), ())),
        preferred_element_type=jnp.float32,
    )
    return lax.psum_scatter(partials.astype(jnp.bfloat16), "head", scatter_dimension=1, tiled=True)


MESH_ID = pl.DeviceIdType.MESH
MASKED = -1e30


def kernel(
    n, q_hbm, k_ref, v_ref, w_ref, lam_ref, len_ref, stride_ref, glob_ref, out_ref,
    q_ref, kv, wown, wother, scores, probs, mine, theirs, obuf,
    kvu_s, kvx_s, kv_r, wu_s, wd_s, wf_s, wx_s, w_r, wy_s, wy_r, sw_s, sw_r, nm_s, nm_r, loc, out_s,
):
    tok, width = q_ref.shape
    dh = width // 2
    rows = w_ref.shape[0]
    half = rows // 2
    nz, nh = n // 2, n // 2
    y, c, h = lax.axis_index("groups"), lax.axis_index("ctx"), lax.axis_index("head")
    z, x = c // 2, c % 2
    has_up, has_down = z + 1 < nz, z >= 1
    up, down, side = {"ctx": c + 2}, {"ctx": c - 2}, {"ctx": c + 1 - 2 * x}
    twin, core = {"groups": 1 - y}, {"head": 1 - h}
    lo = pl.multiple_of(y * half, half)
    hi = pl.multiple_of((1 - y) * half, half)

    barrier = pltpu.get_barrier_semaphore()
    for to in (side, twin, core):
        pl.semaphore_signal(barrier, inc=1, device_id=to, device_id_type=MESH_ID)

    @pl.when(has_up)
    def _():
        pl.semaphore_signal(barrier, inc=1, device_id=up, device_id_type=MESH_ID)

    @pl.when(has_down)
    def _():
        pl.semaphore_signal(barrier, inc=1, device_id=down, device_id_type=MESH_ID)

    loads = [
        pltpu.make_async_copy(src, dst, loc.at[i])
        for i, (src, dst) in enumerate(
            ((k_ref, kv.at[c, 0]), (v_ref, kv.at[c, 1]), (w_ref, wown.at[c]), (q_hbm, q_ref))
        )
    ]
    for load in loads:
        load.start()
    pl.semaphore_wait(barrier, 3 + has_up.astype(jnp.int32) + has_down.astype(jnp.int32))

    def remote(src, dst, send, recv, to):
        return pltpu.make_async_remote_copy(
            src_ref=src, dst_ref=dst, send_sem=send, recv_sem=recv, device_id=to, device_id_type=MESH_ID
        )

    def kv_copy(b, send, to):
        return remote(kv.at[b], kv.at[b], send.at[b], kv_r.at[b], to)

    def w_copy(b, send, to):
        piece = wown.at[b, pl.ds(lo, half)]
        return remote(piece, piece, send.at[b], w_r.at[b], to)

    def y_copy(b, start):
        piece = wown.at[b, pl.ds(start, half)]
        return remote(piece, piece, wy_s.at[b], wy_r.at[b], twin)

    def far_copy(b):
        piece = wown.at[b, pl.ds(hi, half)]
        return remote(piece, piece, wf_s.at[b], wy_r.at[b], down)

    def swap_copy(b, which):
        start = pl.multiple_of(which * half, half)
        slot = b % nh
        return remote(
            wown.at[b, pl.ds(start, half)], wother.at[slot, pl.ds(start, half)],
            sw_s.at[2 * slot + which], sw_r.at[2 * slot + which], core,
        )

    def swap(b, which):
        @pl.when(b // nh == 1 - h)
        def _():
            swap_copy(b, which).start()

    def kv_up(d):
        @pl.when(z >= d)
        def _():
            b = c - 2 * d
            kv_copy(b, kvu_s, up).wait_recv()

            @pl.when(has_up)
            def _():
                kv_copy(b, kvu_s, up).start()

            kv_copy(b, kvx_s, side).start()

    def w_down(d):
        @pl.when(z + d < nz)
        def _():
            b = c + 2 * d
            w_copy(b, wd_s, down).wait_recv()

            @pl.when(has_down)
            def _():
                w_copy(b, wd_s, down).start()

            w_copy(b, wx_s, side).start()
            swap(b, y)
            far_copy(b).wait_recv()

            @pl.when(has_down)
            def _():
                far_copy(b).start()

            swap(b, 1 - y)

    def w_up(d):
        @pl.when(z >= d)
        def _():
            b = c - 2 * d
            w_copy(b, wu_s, up).wait_recv()

            @pl.when(has_up)
            def _():
                w_copy(b, wu_s, up).start()

            y_copy(b, lo).start()
            if d < nz - 1:
                w_copy(b, wx_s, side).start()
            swap(b, y)

    def w_side(d):
        @pl.when((z + d < nz) & (z + d >= 0))
        def _():
            b = 2 * (z + d) + 1 - x
            w_copy(b, wx_s, side).wait_recv()
            y_copy(b, lo).start()
            if d == 2 - nz:
                @pl.when(z == nz - 2)
                def _():
                    w_copy(b, wu_s, up).start()

            swap(b, y)

    def w_twin(b):
        y_copy(b, hi).wait_recv()
        swap(b, 1 - y)

    def kv_side(d):
        @pl.when((z >= d) & ((d > 0) | (x == 1)))
        def _():
            b = 2 * (z - d) + 1 - x
            kv_copy(b, kvx_s, side).wait_recv()

    loads[0].wait()
    loads[1].wait()

    @pl.when(has_up)
    def _():
        kv_copy(c, kvu_s, up).start()

    @pl.when(x == 0)
    def _():
        kv_copy(c, kvx_s, side).start()

    loads[2].wait()

    @pl.when(has_down)
    def _():
        w_copy(c, wd_s, down).start()
        far_copy(c).start()

    w_copy(c, wx_s, side).start()

    @pl.when(has_up)
    def _():
        w_copy(c, wu_s, up).start()

    swap(c, 0)
    swap(c, 1)

    for b in range(1, n):
        @pl.when(c < b)
        def _(b=b):
            kv[b] = jnp.zeros(kv.shape[1:], kv.dtype)

    for d in range(1, nz):
        kv_up(d)
        w_down(d)
        w_up(d)
        w_side(d - 1)
        if d > 1:
            w_side(1 - d)

    scale = 1.0 / math.sqrt(dh)
    lam_init = 0.8 - 0.6 * math.exp(-0.3 * (LAYER - 1))
    lam = [lam_ref[i] for i in range(4)]
    mixing = (
        jnp.exp(jnp.sum(lam[0] * lam[1], -1, keepdims=True))
        - jnp.exp(jnp.sum(lam[2] * lam[3], -1, keepdims=True))
        + lam_init
    )
    blocks_here = tok // BLK

    def score(m):
        q = q_ref[:, m * dh : (m + 1) * dh]
        for b in range(n):
            scores[m, :, b * tok : (b + 1) * tok] = lax.dot_general(
                q, kv[b, 0, :, m * dh : (m + 1) * dh], (((1,), (1,)), ((), ())),
                preferred_element_type=jnp.float32,
            ) * scale

    part = 64

    def soften(i, carry):
        at = pl.multiple_of(i * part, part)
        key_pos = lax.broadcasted_iota(jnp.int32, (1, n * tok), 1)
        key_block = key_pos // BLK
        which = i // (BLK // part)
        block = c * blocks_here + which
        length = len_ref[0]
        stride = [stride_ref[0, j] for j in range(NSTR)]
        for g in range(1, blocks_here):
            length = jnp.where(which == g, len_ref[g], length)
            stride = [jnp.where(which == g, stride_ref[g, j], stride[j]) for j in range(NSTR)]
        floor = block - length
        ok = key_block > floor
        for j in range(NSTR):
            ok = ok | (key_block == stride[j])
        for j in range(GLOB):
            g = glob_ref[j]
            ok = ok | ((key_block == g) & (key_block <= floor))
        last = jnp.where(ok, key_pos, n * tok)
        query = c * tok + at + lax.broadcasted_iota(jnp.int32, (part, 1), 0)
        allowed = last <= query
        maps = []
        for m in range(2):
            s = jnp.where(allowed, scores[m, pl.ds(at, part), :], MASKED)
            e = jnp.exp(s - jnp.max(s, -1, keepdims=True))
            maps.append((e, 1.0 / jnp.sum(e, -1, keepdims=True)))
        (e1, r1), (e2, r2) = maps
        probs[pl.ds(at, part), :] = (e1 * r1 - e2 * (mixing * r2)).astype(probs.dtype)
        return carry

    chunks = tok // part
    w_side(nz - 1)
    for far in range(nz):
        kv_side(far)
    loads[3].wait()
    score(0)
    score(1)
    for i in range(chunks):
        soften(i, 0)
        if i == chunks // 2 - 1:
            w_side(1 - nz)
    mixed = jnp.zeros((tok, width), jnp.float32)
    for b in range(n):
        mixed = mixed + jnp.dot(
            probs[:, b * tok : (b + 1) * tok], kv[b, 1], preferred_element_type=jnp.float32
        )
    normed = mixed * lax.rsqrt(jnp.mean(mixed * mixed, -1, keepdims=True) + 1e-05) * (1.0 - lam_init)
    mine[...] = normed.astype(mine.dtype)
    trade = remote(mine, theirs, nm_s, nm_r, core)
    trade.start()

    def twin_at(d, here):
        @pl.when((z + d < nz) & (z + d >= 0))
        def _():
            w_twin(2 * (z + d) + (x if here else 1 - x))

    for d in range(1, nz):
        twin_at(-d, True)
        twin_at(d - 1, False)
        if d > 1:
            twin_at(1 - d, False)
    twin_at(nz - 1, False)
    twin_at(1 - nz, False)
    trade.wait()

    for i in range(nh):
        j = jnp.where(z >= nz // 2, nh - 1 - i, i)
        for which in range(2):
            swap_copy(h * nh + j, which).wait_recv()
        block = None
        for left, weight in ((mine, wown.at[h * nh + j]), (theirs, wother.at[j])):
            piece = lax.dot_general(
                left[...], weight[...], (((1,), (1,)), ((), ())), preferred_element_type=jnp.float32
            ).astype(jnp.bfloat16).astype(jnp.float32)
            block = piece if block is None else block + piece
        obuf[i] = block.astype(obuf.dtype)
        at = pl.multiple_of(j * rows, rows)
        pltpu.make_async_copy(obuf.at[i], out_ref.at[:, pl.ds(at, rows)], out_s.at[i]).start()

    for b in range(n):
        zb, same = b // 2, (b % 2) == x

        @pl.when(same & has_up & (zb <= z))
        def _(b=b):
            kv_copy(b, kvu_s, up).wait_send()
            w_copy(b, wu_s, up).wait_send()

        @pl.when(same & ((zb < z) | ((zb == z) & (x == 0))))
        def _(b=b):
            kv_copy(b, kvx_s, side).wait_send()

        @pl.when(same & has_down & (zb >= z))
        def _(b=b):
            w_copy(b, wd_s, down).wait_send()
            far_copy(b).wait_send()

        @pl.when(same & ((z < nz - 1) | (zb > 0)))
        def _(b=b):
            w_copy(b, wx_s, side).wait_send()

        if zb == 0:
            @pl.when(jnp.logical_not(same) & (z == nz - 2))
            def _(b=b):
                w_copy(b, wu_s, up).wait_send()

        @pl.when((c != b) & jnp.logical_not(same & (zb > z)))
        def _(b=b):
            y_copy(b, lo).wait_send()

    for j in range(nh):
        for which in range(2):
            swap_copy((1 - h) * nh + j, which).wait_send()
        pltpu.make_async_copy(obuf.at[j], out_ref.at[:, pl.ds(j * rows, rows)], out_s.at[j]).wait()


def fused(queries, keys, values, lambda_vectors, out_weight, local_len, stride_keys, global_blocks):
    n = lax.axis_size("ctx")
    tok, _, width = queries.shape
    rows = out_weight.shape[0]
    nh = n // 2
    vmem = pl.BlockSpec(memory_space=pltpu.VMEM)
    smem = pl.BlockSpec(memory_space=pltpu.SMEM)
    hbm = pl.BlockSpec(memory_space=pl.ANY)
    dma = pltpu.SemaphoreType.DMA
    bf16 = jnp.bfloat16
    return pl.pallas_call(
        functools.partial(kernel, n),
        out_shape=jax.ShapeDtypeStruct((tok, nh * rows), bf16),
        in_specs=[hbm, hbm, hbm, hbm, vmem, smem, smem, smem],
        out_specs=hbm,
        scratch_shapes=[
            pltpu.VMEM((tok, width), bf16),
            pltpu.VMEM((n, 2, tok, width), bf16),
            pltpu.VMEM((n, rows, width), bf16),
            pltpu.VMEM((nh, rows, width), bf16),
            pltpu.VMEM((2, tok, n * tok), jnp.float32),
            pltpu.VMEM((tok, n * tok), bf16),
            pltpu.VMEM((tok, width), bf16),
            pltpu.VMEM((tok, width), bf16),
            pltpu.VMEM((nh, tok, rows), bf16),
        ]
        + [dma((n,)) for _ in range(10)]
        + [dma((n,)), dma((n,)), dma, dma, dma((4,)), dma((nh,))],
        compiler_params=pltpu.CompilerParams(
            collective_id=0, has_side_effects=True, vmem_limit_bytes=60 * 2**20
        ),
    )(
        queries.reshape(tok, width), keys.reshape(tok, width), values.reshape(tok, width),
        out_weight, lambda_vectors, local_len, stride_keys, global_blocks,
    )


def solution(mesh):
    in_specs = (
        P(("groups", "ctx"), "head", None),
        P(("groups", "ctx"), "head", None),
        P(("groups", "ctx"), "head", None),
        P(None, "head", None),
        P("ctx", "head"),
        P(("groups", "ctx")),
        P(("groups", "ctx"), None),
        P("groups"),
    )
    out_specs = P(("groups", "ctx"), "head")
    shape = mesh.shape

    def layer(queries, *rest):
        per_device = queries.shape[0] // (shape["groups"] * shape["ctx"])
        score_bytes = 8 * per_device * per_device * shape["ctx"]
        fits = score_bytes <= 8 * 2**20 and shape["groups"] == 2 and shape["head"] == 2
        chosen = fused if fits and shape["ctx"] % 2 == 0 and shape["ctx"] >= 4 else body
        mapped = jax.shard_map(chosen, mesh=mesh, in_specs=in_specs, out_specs=out_specs, check_vma=False)
        return mapped(queries, *rest)

    return layer
```

```python
import functools
import math

import jax
import jax.numpy as jnp
from jax import lax
from jax.experimental import pallas as pl
from jax.experimental.pallas import tpu as pltpu
from jax.sharding import PartitionSpec as P

BLK = 128
NSTR = 3
GLOB = 4
PIECES = 2
LAYER = 12


def shifted(shard, axis, by):
    length = lax.axis_size(axis)
    pairs = [(i, i + by) for i in range(length) if 0 <= i + by < length]
    return lax.ppermute(shard, axis, pairs)


def from_root(value, axis, source):
    kept = jnp.where(lax.axis_index(axis) == source, value, 0).astype(value.dtype)
    return lax.psum(kept, axis)


def masked_softmax(scores, allowed):
    masked_scores = jnp.where(allowed, scores, -jnp.inf)
    highest = jnp.max(masked_scores, -1, keepdims=True)
    raised = jnp.where(allowed, jnp.exp(masked_scores - highest), 0.0)
    return raised / jnp.sum(raised, -1, keepdims=True)


def body(queries, keys, values, lambda_vectors, out_weight, local_len, stride_keys, global_blocks):
    tok_dev, heads_here, double_width = queries.shape
    head_dim = double_width // 2
    blocks_here = tok_dev // BLK
    ctx_count = lax.axis_size("ctx")
    ctx_pos = lax.axis_index("ctx")
    step_dev = ctx_count // (NSTR + 1)
    lam_init = 0.8 - 0.6 * math.exp(-0.3 * (LAYER - 1))
    mixing = (
        jnp.exp(jnp.sum(lambda_vectors[0] * lambda_vectors[1], -1))
        - jnp.exp(jnp.sum(lambda_vectors[2] * lambda_vectors[3], -1))
        + lam_init
    )
    key_vals = jnp.concatenate((keys, values), axis=-1)
    prev_data = shifted(key_vals, "ctx", 1)
    remote = []
    moving = key_vals
    for slot_pos in range(NSTR):
        moving = shifted(moving, "ctx", step_dev)
        remote.append(moving)
    global_list = []
    for global_pos in range(GLOB):
        block_id = global_blocks[global_pos]
        owner_pos = block_id // blocks_here
        first_row = block_id % blocks_here * BLK
        block_data = lax.dynamic_slice_in_dim(key_vals, first_row, BLK, 0)
        global_list.append(from_root(block_data, "ctx", owner_pos))
    global_data = jnp.concatenate(global_list, 0)
    candidates = jnp.concatenate([key_vals, prev_data] + remote + [global_data], 0)
    cand_keys = candidates[..., :double_width]
    cand_values = candidates[..., double_width:]
    rows_here = jnp.arange(tok_dev, dtype=jnp.int32)
    query_pos = ctx_pos * tok_dev + rows_here
    query_block = query_pos // BLK
    owner_mask = (rows_here // BLK)[:, None] == jnp.arange(blocks_here, dtype=jnp.int32)[None, :]
    length = jnp.sum(jnp.where(owner_mask, local_len[None, :], 0), 1)
    stride_rows = jnp.sum(jnp.where(owner_mask[:, :, None], stride_keys[None, :, :], 0), 1)
    window_floor = query_block - length
    own_block = ctx_pos * blocks_here + rows_here // BLK
    own_ok = (own_block[None, :] > window_floor[:, None]) & (
        query_pos[None, :] - rows_here[:, None] + rows_here[None, :] <= query_pos[:, None]
    )
    prev_block = (ctx_pos - 1) * blocks_here + rows_here // BLK
    prev_ok = (prev_block[None, :] > window_floor[:, None]) & (prev_block[None, :] >= 0)
    masks = [own_ok, prev_ok]
    for slot_pos in range(NSTR):
        far_block = (ctx_pos - (slot_pos + 1) * step_dev) * blocks_here + rows_here // BLK
        listed = stride_rows[:, slot_pos][:, None]
        masks.append((listed == far_block[None, :]) & (listed >= 0))
    in_stride = jnp.any(stride_rows[:, :, None] == global_blocks[None, None, :], 1)
    global_key = jnp.repeat(global_blocks, BLK)
    global_ok = (global_key[None, :] <= window_floor[:, None]) & jnp.logical_not(
        jnp.repeat(in_stride, BLK, axis=1)
    )
    masks.append(global_ok)
    allowed = jnp.concatenate(masks, 1)
    score_scale = 1.0 / math.sqrt(head_dim)
    scores_one = (
        jnp.einsum(
            "qhd,khd->hqk",
            queries[..., :head_dim],
            cand_keys[..., :head_dim],
            preferred_element_type=jnp.float32,
        )
        * score_scale
    )
    scores_two = (
        jnp.einsum(
            "qhd,khd->hqk",
            queries[..., head_dim:],
            cand_keys[..., head_dim:],
            preferred_element_type=jnp.float32,
        )
        * score_scale
    )
    attn_one = masked_softmax(scores_one, allowed)
    attn_two = masked_softmax(scores_two, allowed)
    weights = (attn_one - mixing[:, None, None] * attn_two).astype(jnp.bfloat16)
    mixed_out = jnp.einsum("hqk,khe->qhe", weights, cand_values, preferred_element_type=jnp.float32)
    normed = (
        mixed_out
        * lax.rsqrt(jnp.mean(mixed_out * mixed_out, -1, keepdims=True) + 1e-05)
        * (1.0 - lam_init)
    ).astype(jnp.bfloat16)
    flat_heads = normed.reshape(tok_dev, heads_here * double_width)
    partials = lax.dot_general(
        flat_heads,
        lax.all_gather(out_weight, "ctx", axis=0, tiled=True),
        (((1,), (1,)), ((), ())),
        preferred_element_type=jnp.float32,
    )
    return lax.psum_scatter(partials.astype(jnp.bfloat16), "head", scatter_dimension=1, tiled=True)


MESH_ID = pl.DeviceIdType.MESH
MASKED = -1e30


def kernel(
    n, q_hbm, k_ref, v_ref, w_ref, lam_ref, len_ref, stride_ref, glob_ref, out_ref,
    q_ref, kv, wown, wother, scores, probs, mine, theirs, obuf,
    kvu_s, kvx_s, kv_r, wu_s, wd_s, wf_s, wx_s, w_r, wy_s, wy_r, sw_s, sw_r, nm_s, nm_r, loc, out_s,
):
    tok, width = q_ref.shape
    dh = width // 2
    rows = w_ref.shape[0]
    half = rows // 2
    size = half // PIECES
    nz, nh = n // 2, n // 2
    y, c, h = lax.axis_index("groups"), lax.axis_index("ctx"), lax.axis_index("head")
    z, x = c // 2, c % 2
    has_up, has_down = z + 1 < nz, z >= 1
    up, down, side = {"ctx": c + 2}, {"ctx": c - 2}, {"ctx": c + 1 - 2 * x}
    twin, core = {"groups": 1 - y}, {"head": 1 - h}
    lo, hi = y, 1 - y

    def rows_of(which, p):
        return pl.ds(pl.multiple_of(which * half + p * size, size), size)

    barrier = pltpu.get_barrier_semaphore()
    for to in (side, twin, core):
        pl.semaphore_signal(barrier, inc=1, device_id=to, device_id_type=MESH_ID)

    @pl.when(has_up)
    def _():
        pl.semaphore_signal(barrier, inc=1, device_id=up, device_id_type=MESH_ID)

    @pl.when(has_down)
    def _():
        pl.semaphore_signal(barrier, inc=1, device_id=down, device_id_type=MESH_ID)

    loads = [
        pltpu.make_async_copy(src, dst, loc.at[i])
        for i, (src, dst) in enumerate(
            ((k_ref, kv.at[c, 0]), (v_ref, kv.at[c, 1]), (w_ref, wown.at[c]), (q_hbm, q_ref))
        )
    ]
    for load in loads:
        load.start()
    pl.semaphore_wait(barrier, 3 + has_up.astype(jnp.int32) + has_down.astype(jnp.int32))

    def remote(src, dst, send, recv, to):
        return pltpu.make_async_remote_copy(
            src_ref=src, dst_ref=dst, send_sem=send, recv_sem=recv, device_id=to, device_id_type=MESH_ID
        )

    def kv_copy(b, send, to):
        return remote(kv.at[b], kv.at[b], send.at[b], kv_r.at[b], to)

    def w_copy(b, p, send, to):
        piece = wown.at[b, rows_of(lo, p)]
        return remote(piece, piece, send.at[b, p], w_r.at[b, p], to)

    def y_copy(b, p, which):
        piece = wown.at[b, rows_of(which, p)]
        return remote(piece, piece, wy_s.at[b, p], wy_r.at[b, p], twin)

    def far_copy(b, p):
        piece = wown.at[b, rows_of(hi, p)]
        return remote(piece, piece, wf_s.at[b, p], wy_r.at[b, p], down)

    def swap_copy(b, which, p):
        slot = b % nh
        return remote(
            wown.at[b, rows_of(which, p)], wother.at[slot, rows_of(which, p)],
            sw_s.at[2 * slot + which, p], sw_r.at[2 * slot + which, p], core,
        )

    def swap(b, which, p):
        @pl.when(b // nh == 1 - h)
        def _():
            swap_copy(b, which, p).start()

    def kv_up(d):
        @pl.when(z >= d)
        def _():
            b = c - 2 * d
            kv_copy(b, kvu_s, up).wait_recv()

            @pl.when(has_up)
            def _():
                kv_copy(b, kvu_s, up).start()

            kv_copy(b, kvx_s, side).start()

    def w_down(d):
        @pl.when(z + d < nz)
        def _():
            b = c + 2 * d
            for p in range(PIECES):
                w_copy(b, p, wd_s, down).wait_recv()

                @pl.when(has_down)
                def _():
                    w_copy(b, p, wd_s, down).start()

                w_copy(b, p, wx_s, side).start()
                swap(b, lo, p)
            for p in range(PIECES):
                far_copy(b, p).wait_recv()

                @pl.when(has_down)
                def _():
                    far_copy(b, p).start()

                swap(b, hi, p)

    def w_up(d):
        @pl.when(z >= d)
        def _():
            b = c - 2 * d
            for p in range(PIECES):
                w_copy(b, p, wu_s, up).wait_recv()

                @pl.when(has_up)
                def _():
                    w_copy(b, p, wu_s, up).start()

                y_copy(b, p, lo).start()
                if d < nz - 1:
                    w_copy(b, p, wx_s, side).start()
                swap(b, lo, p)

    def w_side(d):
        @pl.when((z + d < nz) & (z + d >= 0))
        def _():
            b = 2 * (z + d) + 1 - x
            for p in range(PIECES):
                w_copy(b, p, wx_s, side).wait_recv()
                y_copy(b, p, lo).start()
                if d == 2 - nz:
                    @pl.when(z == nz - 2)
                    def _():
                        w_copy(b, p, wu_s, up).start()

                swap(b, lo, p)

    def w_twin(b):
        for p in range(PIECES):
            y_copy(b, p, hi).wait_recv()
            swap(b, hi, p)

    def kv_side(d):
        @pl.when((z >= d) & ((d > 0) | (x == 1)))
        def _():
            b = 2 * (z - d) + 1 - x
            kv_copy(b, kvx_s, side).wait_recv()

    loads[2].wait()
    for p in range(PIECES):
        @pl.when(has_up)
        def _():
            w_copy(c, p, wu_s, up).start()

        w_copy(c, p, wx_s, side).start()

        @pl.when(has_down)
        def _():
            w_copy(c, p, wd_s, down).start()

    loads[0].wait()
    loads[1].wait()

    @pl.when(has_up)
    def _():
        kv_copy(c, kvu_s, up).start()

    @pl.when(x == 0)
    def _():
        kv_copy(c, kvx_s, side).start()

    for p in range(PIECES):
        @pl.when(has_down)
        def _():
            far_copy(c, p).start()

        swap(c, 0, p)
        swap(c, 1, p)

    for b in range(1, n):
        @pl.when(c < b)
        def _(b=b):
            kv[b] = jnp.zeros(kv.shape[1:], kv.dtype)

    for d in range(1, nz):
        w_up(d)
        w_side(d - 1)
        if d > 1:
            w_side(1 - d)
        kv_up(d)
        w_down(d)

    scale = 1.0 / math.sqrt(dh)
    lam_init = 0.8 - 0.6 * math.exp(-0.3 * (LAYER - 1))
    lam = [lam_ref[i] for i in range(4)]
    mixing = (
        jnp.exp(jnp.sum(lam[0] * lam[1], -1, keepdims=True))
        - jnp.exp(jnp.sum(lam[2] * lam[3], -1, keepdims=True))
        + lam_init
    )
    blocks_here = tok // BLK

    def score(m):
        q = q_ref[:, m * dh : (m + 1) * dh]
        for b in range(n):
            scores[m, :, b * tok : (b + 1) * tok] = lax.dot_general(
                q, kv[b, 0, :, m * dh : (m + 1) * dh], (((1,), (1,)), ((), ())),
                preferred_element_type=jnp.float32,
            ) * scale

    part = 64

    def soften(i, carry):
        at = pl.multiple_of(i * part, part)
        key_pos = lax.broadcasted_iota(jnp.int32, (1, n * tok), 1)
        key_block = key_pos // BLK
        which = i // (BLK // part)
        block = c * blocks_here + which
        length = len_ref[0]
        stride = [stride_ref[0, j] for j in range(NSTR)]
        for g in range(1, blocks_here):
            length = jnp.where(which == g, len_ref[g], length)
            stride = [jnp.where(which == g, stride_ref[g, j], stride[j]) for j in range(NSTR)]
        floor = block - length
        ok = key_block > floor
        for j in range(NSTR):
            ok = ok | (key_block == stride[j])
        for j in range(GLOB):
            g = glob_ref[j]
            ok = ok | ((key_block == g) & (key_block <= floor))
        last = jnp.where(ok, key_pos, n * tok)
        query = c * tok + at + lax.broadcasted_iota(jnp.int32, (part, 1), 0)
        allowed = last <= query
        maps = []
        for m in range(2):
            s = jnp.where(allowed, scores[m, pl.ds(at, part), :], MASKED)
            e = jnp.exp(s - jnp.max(s, -1, keepdims=True))
            maps.append((e, 1.0 / jnp.sum(e, -1, keepdims=True)))
        (e1, r1), (e2, r2) = maps
        probs[pl.ds(at, part), :] = (e1 * r1 - e2 * (mixing * r2)).astype(probs.dtype)
        return carry

    chunks = tok // part
    w_side(nz - 1)
    for far in range(nz):
        kv_side(far)
    loads[3].wait()
    score(0)
    score(1)
    for i in range(chunks):
        soften(i, 0)
        if i == chunks // 2 - 1:
            w_side(1 - nz)
    mixed = jnp.zeros((tok, width), jnp.float32)
    for b in range(n):
        mixed = mixed + jnp.dot(
            probs[:, b * tok : (b + 1) * tok], kv[b, 1], preferred_element_type=jnp.float32
        )
    normed = mixed * lax.rsqrt(jnp.mean(mixed * mixed, -1, keepdims=True) + 1e-05) * (1.0 - lam_init)
    mine[...] = normed.astype(mine.dtype)
    trade = remote(mine, theirs, nm_s, nm_r, core)
    trade.start()

    def twin_at(d, here):
        @pl.when((z + d < nz) & (z + d >= 0))
        def _():
            w_twin(2 * (z + d) + (x if here else 1 - x))

    for d in range(1, nz):
        twin_at(-d, True)
        twin_at(d - 1, False)
        if d > 1:
            twin_at(1 - d, False)
    twin_at(nz - 1, False)
    twin_at(1 - nz, False)
    trade.wait()

    for i in range(nh):
        j = jnp.where(z >= nz // 2, nh - 1 - i, i)
        for which in range(2):
            for p in range(PIECES):
                swap_copy(h * nh + j, which, p).wait_recv()
        block = None
        for left, weight in ((mine, wown.at[h * nh + j]), (theirs, wother.at[j])):
            piece = lax.dot_general(
                left[...], weight[...], (((1,), (1,)), ((), ())), preferred_element_type=jnp.float32
            ).astype(jnp.bfloat16).astype(jnp.float32)
            block = piece if block is None else block + piece
        obuf[i] = block.astype(obuf.dtype)
        at = pl.multiple_of(j * rows, rows)
        pltpu.make_async_copy(obuf.at[i], out_ref.at[:, pl.ds(at, rows)], out_s.at[i]).start()

    for b in range(n):
        zb, same = b // 2, (b % 2) == x

        @pl.when(same & has_up & (zb <= z))
        def _(b=b):
            kv_copy(b, kvu_s, up).wait_send()
            for p in range(PIECES):
                w_copy(b, p, wu_s, up).wait_send()

        @pl.when(same & ((zb < z) | ((zb == z) & (x == 0))))
        def _(b=b):
            kv_copy(b, kvx_s, side).wait_send()

        @pl.when(same & has_down & (zb >= z))
        def _(b=b):
            for p in range(PIECES):
                w_copy(b, p, wd_s, down).wait_send()
            for p in range(PIECES):
                far_copy(b, p).wait_send()

        @pl.when(same & ((z < nz - 1) | (zb > 0)))
        def _(b=b):
            for p in range(PIECES):
                w_copy(b, p, wx_s, side).wait_send()

        if zb == 0:
            @pl.when(jnp.logical_not(same) & (z == nz - 2))
            def _(b=b):
                for p in range(PIECES):
                    w_copy(b, p, wu_s, up).wait_send()

        @pl.when((c != b) & jnp.logical_not(same & (zb > z)))
        def _(b=b):
            for p in range(PIECES):
                y_copy(b, p, lo).wait_send()

    for j in range(nh):
        for which in range(2):
            for p in range(PIECES):
                swap_copy((1 - h) * nh + j, which, p).wait_send()
        pltpu.make_async_copy(obuf.at[j], out_ref.at[:, pl.ds(j * rows, rows)], out_s.at[j]).wait()


def fused(queries, keys, values, lambda_vectors, out_weight, local_len, stride_keys, global_blocks):
    n = lax.axis_size("ctx")
    tok, _, width = queries.shape
    rows = out_weight.shape[0]
    nh = n // 2
    vmem = pl.BlockSpec(memory_space=pltpu.VMEM)
    smem = pl.BlockSpec(memory_space=pltpu.SMEM)
    hbm = pl.BlockSpec(memory_space=pl.ANY)
    dma = pltpu.SemaphoreType.DMA
    bf16 = jnp.bfloat16
    return pl.pallas_call(
        functools.partial(kernel, n),
        out_shape=jax.ShapeDtypeStruct((tok, nh * rows), bf16),
        in_specs=[hbm, hbm, hbm, hbm, vmem, smem, smem, smem],
        out_specs=hbm,
        scratch_shapes=[
            pltpu.VMEM((tok, width), bf16),
            pltpu.VMEM((n, 2, tok, width), bf16),
            pltpu.VMEM((n, rows, width), bf16),
            pltpu.VMEM((nh, rows, width), bf16),
            pltpu.VMEM((2, tok, n * tok), jnp.float32),
            pltpu.VMEM((tok, n * tok), bf16),
            pltpu.VMEM((tok, width), bf16),
            pltpu.VMEM((tok, width), bf16),
            pltpu.VMEM((nh, tok, rows), bf16),
        ]
        + [dma((n,))] * 3
        + [dma((n, PIECES))] * 7
        + [dma((n, PIECES))] * 2
        + [dma, dma, dma((4,)), dma((nh,))],
        compiler_params=pltpu.CompilerParams(
            collective_id=0, has_side_effects=True, vmem_limit_bytes=60 * 2**20
        ),
    )(
        queries.reshape(tok, width), keys.reshape(tok, width), values.reshape(tok, width),
        out_weight, lambda_vectors, local_len, stride_keys, global_blocks,
    )


def solution(mesh):
    in_specs = (
        P(("groups", "ctx"), "head", None),
        P(("groups", "ctx"), "head", None),
        P(("groups", "ctx"), "head", None),
        P(None, "head", None),
        P("ctx", "head"),
        P(("groups", "ctx")),
        P(("groups", "ctx"), None),
        P("groups"),
    )
    out_specs = P(("groups", "ctx"), "head")
    shape = mesh.shape

    def layer(queries, *rest):
        per_device = queries.shape[0] // (shape["groups"] * shape["ctx"])
        score_bytes = 8 * per_device * per_device * shape["ctx"]
        fits = score_bytes <= 8 * 2**20 and shape["groups"] == 2 and shape["head"] == 2
        chosen = fused if fits and shape["ctx"] % 2 == 0 and shape["ctx"] >= 4 else body
        mapped = jax.shard_map(chosen, mesh=mesh, in_specs=in_specs, out_specs=out_specs, check_vma=False)
        return mapped(queries, *rest)

    return layer
```

```python
import functools
import math

import jax
import jax.numpy as jnp
from jax import lax
from jax.experimental import pallas as pl
from jax.experimental.pallas import tpu as pltpu
from jax.sharding import PartitionSpec as P

BLK = 128
NSTR = 3
GLOB = 4
PIECES = 2
LAYER = 12


def shifted(shard, axis, by):
    length = lax.axis_size(axis)
    pairs = [(i, i + by) for i in range(length) if 0 <= i + by < length]
    return lax.ppermute(shard, axis, pairs)


def from_root(value, axis, source):
    kept = jnp.where(lax.axis_index(axis) == source, value, 0).astype(value.dtype)
    return lax.psum(kept, axis)


def masked_softmax(scores, allowed):
    masked_scores = jnp.where(allowed, scores, -jnp.inf)
    highest = jnp.max(masked_scores, -1, keepdims=True)
    raised = jnp.where(allowed, jnp.exp(masked_scores - highest), 0.0)
    return raised / jnp.sum(raised, -1, keepdims=True)


def body(queries, keys, values, lambda_vectors, out_weight, local_len, stride_keys, global_blocks):
    tok_dev, heads_here, double_width = queries.shape
    head_dim = double_width // 2
    blocks_here = tok_dev // BLK
    ctx_count = lax.axis_size("ctx")
    ctx_pos = lax.axis_index("ctx")
    step_dev = ctx_count // (NSTR + 1)
    lam_init = 0.8 - 0.6 * math.exp(-0.3 * (LAYER - 1))
    mixing = (
        jnp.exp(jnp.sum(lambda_vectors[0] * lambda_vectors[1], -1))
        - jnp.exp(jnp.sum(lambda_vectors[2] * lambda_vectors[3], -1))
        + lam_init
    )
    key_vals = jnp.concatenate((keys, values), axis=-1)
    prev_data = shifted(key_vals, "ctx", 1)
    remote = []
    moving = key_vals
    for slot_pos in range(NSTR):
        moving = shifted(moving, "ctx", step_dev)
        remote.append(moving)
    global_list = []
    for global_pos in range(GLOB):
        block_id = global_blocks[global_pos]
        owner_pos = block_id // blocks_here
        first_row = block_id % blocks_here * BLK
        block_data = lax.dynamic_slice_in_dim(key_vals, first_row, BLK, 0)
        global_list.append(from_root(block_data, "ctx", owner_pos))
    global_data = jnp.concatenate(global_list, 0)
    candidates = jnp.concatenate([key_vals, prev_data] + remote + [global_data], 0)
    cand_keys = candidates[..., :double_width]
    cand_values = candidates[..., double_width:]
    rows_here = jnp.arange(tok_dev, dtype=jnp.int32)
    query_pos = ctx_pos * tok_dev + rows_here
    query_block = query_pos // BLK
    owner_mask = (rows_here // BLK)[:, None] == jnp.arange(blocks_here, dtype=jnp.int32)[None, :]
    length = jnp.sum(jnp.where(owner_mask, local_len[None, :], 0), 1)
    stride_rows = jnp.sum(jnp.where(owner_mask[:, :, None], stride_keys[None, :, :], 0), 1)
    window_floor = query_block - length
    own_block = ctx_pos * blocks_here + rows_here // BLK
    own_ok = (own_block[None, :] > window_floor[:, None]) & (
        query_pos[None, :] - rows_here[:, None] + rows_here[None, :] <= query_pos[:, None]
    )
    prev_block = (ctx_pos - 1) * blocks_here + rows_here // BLK
    prev_ok = (prev_block[None, :] > window_floor[:, None]) & (prev_block[None, :] >= 0)
    masks = [own_ok, prev_ok]
    for slot_pos in range(NSTR):
        far_block = (ctx_pos - (slot_pos + 1) * step_dev) * blocks_here + rows_here // BLK
        listed = stride_rows[:, slot_pos][:, None]
        masks.append((listed == far_block[None, :]) & (listed >= 0))
    in_stride = jnp.any(stride_rows[:, :, None] == global_blocks[None, None, :], 1)
    global_key = jnp.repeat(global_blocks, BLK)
    global_ok = (global_key[None, :] <= window_floor[:, None]) & jnp.logical_not(
        jnp.repeat(in_stride, BLK, axis=1)
    )
    masks.append(global_ok)
    allowed = jnp.concatenate(masks, 1)
    score_scale = 1.0 / math.sqrt(head_dim)
    scores_one = (
        jnp.einsum(
            "qhd,khd->hqk",
            queries[..., :head_dim],
            cand_keys[..., :head_dim],
            preferred_element_type=jnp.float32,
        )
        * score_scale
    )
    scores_two = (
        jnp.einsum(
            "qhd,khd->hqk",
            queries[..., head_dim:],
            cand_keys[..., head_dim:],
            preferred_element_type=jnp.float32,
        )
        * score_scale
    )
    attn_one = masked_softmax(scores_one, allowed)
    attn_two = masked_softmax(scores_two, allowed)
    weights = (attn_one - mixing[:, None, None] * attn_two).astype(jnp.bfloat16)
    mixed_out = jnp.einsum("hqk,khe->qhe", weights, cand_values, preferred_element_type=jnp.float32)
    normed = (
        mixed_out
        * lax.rsqrt(jnp.mean(mixed_out * mixed_out, -1, keepdims=True) + 1e-05)
        * (1.0 - lam_init)
    ).astype(jnp.bfloat16)
    flat_heads = normed.reshape(tok_dev, heads_here * double_width)
    partials = lax.dot_general(
        flat_heads,
        lax.all_gather(out_weight, "ctx", axis=0, tiled=True),
        (((1,), (1,)), ((), ())),
        preferred_element_type=jnp.float32,
    )
    return lax.psum_scatter(partials.astype(jnp.bfloat16), "head", scatter_dimension=1, tiled=True)


MESH_ID = pl.DeviceIdType.MESH
MASKED = -1e30


def kernel(
    n, q_hbm, k_ref, v_ref, w_ref, lam_ref, len_ref, stride_ref, glob_ref, out_ref,
    q_ref, kv, wown, wother, scores, probs, mine, theirs, obuf,
    kvu_s, kvx_s, kv_r, wu_s, wd_s, wf_s, wx_s, w_r, wy_s, wy_r, sw_s, sw_r, nm_s, nm_r, loc, out_s,
):
    tok, width = q_ref.shape
    dh = width // 2
    rows = w_ref.shape[0]
    half = rows // 2
    size = half // PIECES
    nz, nh = n // 2, n // 2
    y, c, h = lax.axis_index("groups"), lax.axis_index("ctx"), lax.axis_index("head")
    z, x = c // 2, c % 2
    has_up, has_down = z + 1 < nz, z >= 1
    up, down, side = {"ctx": c + 2}, {"ctx": c - 2}, {"ctx": c + 1 - 2 * x}
    twin, core = {"groups": 1 - y}, {"head": 1 - h}
    lo, hi = y, 1 - y

    def rows_of(which, p):
        return pl.ds(pl.multiple_of(which * half + p * size, size), size)

    barrier = pltpu.get_barrier_semaphore()
    for to in (side, twin, core):
        pl.semaphore_signal(barrier, inc=1, device_id=to, device_id_type=MESH_ID)

    @pl.when(has_up)
    def _():
        pl.semaphore_signal(barrier, inc=1, device_id=up, device_id_type=MESH_ID)

    @pl.when(has_down)
    def _():
        pl.semaphore_signal(barrier, inc=1, device_id=down, device_id_type=MESH_ID)

    loads = [
        pltpu.make_async_copy(src, dst, loc.at[i])
        for i, (src, dst) in enumerate(
            ((k_ref, kv.at[c, 0]), (v_ref, kv.at[c, 1]), (w_ref, wown.at[c]), (q_hbm, q_ref))
        )
    ]
    for load in loads:
        load.start()
    pl.semaphore_wait(barrier, 3 + has_up.astype(jnp.int32) + has_down.astype(jnp.int32))

    def remote(src, dst, send, recv, to):
        return pltpu.make_async_remote_copy(
            src_ref=src, dst_ref=dst, send_sem=send, recv_sem=recv, device_id=to, device_id_type=MESH_ID
        )

    def kv_copy(b, send, to):
        return remote(kv.at[b], kv.at[b], send.at[b], kv_r.at[b], to)

    def w_copy(b, p, send, to):
        piece = wown.at[b, rows_of(lo, p)]
        return remote(piece, piece, send.at[b, p], w_r.at[b, p], to)

    def y_copy(b, p, which):
        piece = wown.at[b, rows_of(which, p)]
        return remote(piece, piece, wy_s.at[b, p], wy_r.at[b, p], twin)

    def far_copy(b, p):
        piece = wown.at[b, rows_of(hi, p)]
        return remote(piece, piece, wf_s.at[b, p], wy_r.at[b, p], down)

    def swap_copy(b, which, p):
        slot = b % nh
        return remote(
            wown.at[b, rows_of(which, p)], wother.at[slot, rows_of(which, p)],
            sw_s.at[2 * slot + which, p], sw_r.at[2 * slot + which, p], core,
        )

    def swap(b, which, p):
        @pl.when(b // nh == 1 - h)
        def _():
            swap_copy(b, which, p).start()

    def kv_up(d):
        @pl.when(z >= d)
        def _():
            b = c - 2 * d
            kv_copy(b, kvu_s, up).wait_recv()

            @pl.when(has_up)
            def _():
                kv_copy(b, kvu_s, up).start()

            kv_copy(b, kvx_s, side).start()

    def w_down(d):
        @pl.when(z + d < nz)
        def _():
            b = c + 2 * d
            for p in range(PIECES):
                w_copy(b, p, wd_s, down).wait_recv()

                @pl.when(has_down)
                def _():
                    w_copy(b, p, wd_s, down).start()

                w_copy(b, p, wx_s, side).start()
                swap(b, lo, p)

    def far_down(d):
        @pl.when(z + d < nz)
        def _():
            b = c + 2 * d
            for p in range(PIECES):
                far_copy(b, p).wait_recv()

                @pl.when(has_down)
                def _():
                    far_copy(b, p).start()

                swap(b, hi, p)

    def w_up(d):
        @pl.when(z >= d)
        def _():
            b = c - 2 * d
            for p in range(PIECES):
                w_copy(b, p, wu_s, up).wait_recv()

                @pl.when(has_up)
                def _():
                    w_copy(b, p, wu_s, up).start()

                y_copy(b, p, lo).start()
                if d < nz - 1:
                    w_copy(b, p, wx_s, side).start()
                swap(b, lo, p)

    def w_side(d):
        @pl.when((z + d < nz) & (z + d >= 0))
        def _():
            b = 2 * (z + d) + 1 - x
            for p in range(PIECES):
                w_copy(b, p, wx_s, side).wait_recv()
                y_copy(b, p, lo).start()
                if d == 2 - nz:
                    @pl.when(z == nz - 2)
                    def _():
                        w_copy(b, p, wu_s, up).start()

                swap(b, lo, p)

    def w_twin(b):
        for p in range(PIECES):
            y_copy(b, p, hi).wait_recv()
            swap(b, hi, p)

    def kv_side(d):
        @pl.when((z >= d) & ((d > 0) | (x == 1)))
        def _():
            b = 2 * (z - d) + 1 - x
            kv_copy(b, kvx_s, side).wait_recv()

    loads[2].wait()
    for p in range(PIECES):
        @pl.when(has_up)
        def _():
            w_copy(c, p, wu_s, up).start()

        w_copy(c, p, wx_s, side).start()

        @pl.when(has_down)
        def _():
            w_copy(c, p, wd_s, down).start()

    loads[0].wait()
    loads[1].wait()

    @pl.when(has_up)
    def _():
        kv_copy(c, kvu_s, up).start()

    @pl.when(x == 0)
    def _():
        kv_copy(c, kvx_s, side).start()

    for p in range(PIECES):
        @pl.when(has_down)
        def _():
            far_copy(c, p).start()

        swap(c, 0, p)
        swap(c, 1, p)

    for b in range(1, n):
        @pl.when(c < b)
        def _(b=b):
            kv[b] = jnp.zeros(kv.shape[1:], kv.dtype)

    for d in range(1, nz):
        w_down(d)
        if d > 1:
            kv_up(d)
        w_up(d)
        if d == 1:
            kv_up(d)
        w_side(d - 1)
        if d > 1:
            w_side(1 - d)
        far_down(d)

    scale = 1.0 / math.sqrt(dh)
    lam_init = 0.8 - 0.6 * math.exp(-0.3 * (LAYER - 1))
    lam = [lam_ref[i] for i in range(4)]
    mixing = (
        jnp.exp(jnp.sum(lam[0] * lam[1], -1, keepdims=True))
        - jnp.exp(jnp.sum(lam[2] * lam[3], -1, keepdims=True))
        + lam_init
    )
    blocks_here = tok // BLK

    def score(m):
        q = q_ref[:, m * dh : (m + 1) * dh]
        for b in range(n):
            scores[m, :, b * tok : (b + 1) * tok] = lax.dot_general(
                q, kv[b, 0, :, m * dh : (m + 1) * dh], (((1,), (1,)), ((), ())),
                preferred_element_type=jnp.float32,
            ) * scale

    part = 64

    def soften(i, carry):
        at = pl.multiple_of(i * part, part)
        key_pos = lax.broadcasted_iota(jnp.int32, (1, n * tok), 1)
        key_block = key_pos // BLK
        which = i // (BLK // part)
        block = c * blocks_here + which
        length = len_ref[0]
        stride = [stride_ref[0, j] for j in range(NSTR)]
        for g in range(1, blocks_here):
            length = jnp.where(which == g, len_ref[g], length)
            stride = [jnp.where(which == g, stride_ref[g, j], stride[j]) for j in range(NSTR)]
        floor = block - length
        ok = key_block > floor
        for j in range(NSTR):
            ok = ok | (key_block == stride[j])
        for j in range(GLOB):
            g = glob_ref[j]
            ok = ok | ((key_block == g) & (key_block <= floor))
        last = jnp.where(ok, key_pos, n * tok)
        query = c * tok + at + lax.broadcasted_iota(jnp.int32, (part, 1), 0)
        allowed = last <= query
        maps = []
        for m in range(2):
            s = jnp.where(allowed, scores[m, pl.ds(at, part), :], MASKED)
            e = jnp.exp(s - jnp.max(s, -1, keepdims=True))
            maps.append((e, 1.0 / jnp.sum(e, -1, keepdims=True)))
        (e1, r1), (e2, r2) = maps
        probs[pl.ds(at, part), :] = (e1 * r1 - e2 * (mixing * r2)).astype(probs.dtype)
        return carry

    chunks = tok // part
    w_side(nz - 1)
    for far in range(nz):
        kv_side(far)
    loads[3].wait()
    score(0)
    score(1)
    for i in range(chunks):
        soften(i, 0)
        if i == chunks // 2 - 1:
            w_side(1 - nz)
    mixed = jnp.zeros((tok, width), jnp.float32)
    for b in range(n):
        mixed = mixed + jnp.dot(
            probs[:, b * tok : (b + 1) * tok], kv[b, 1], preferred_element_type=jnp.float32
        )
    normed = mixed * lax.rsqrt(jnp.mean(mixed * mixed, -1, keepdims=True) + 1e-05) * (1.0 - lam_init)
    mine[...] = normed.astype(mine.dtype)
    trade = remote(mine, theirs, nm_s, nm_r, core)
    trade.start()

    def twin_at(d, here):
        @pl.when((z + d < nz) & (z + d >= 0))
        def _():
            w_twin(2 * (z + d) + (x if here else 1 - x))

    for d in range(1, nz):
        twin_at(-d, True)
        twin_at(d - 1, False)
        if d > 1:
            twin_at(1 - d, False)
    trade.wait()

    for i in range(nh):
        if i == nh - 1:
            twin_at(nz - 1, False)
            twin_at(1 - nz, False)
        pair = jnp.where(z >= nz // 2, nh // 2 - 1 - i // 2, i // 2)
        j = 2 * pair + (x if i % 2 == 0 else 1 - x)
        for which in range(2):
            for p in range(PIECES):
                swap_copy(h * nh + j, which, p).wait_recv()
        block = None
        for left, weight in ((mine, wown.at[h * nh + j]), (theirs, wother.at[j])):
            piece = lax.dot_general(
                left[...], weight[...], (((1,), (1,)), ((), ())), preferred_element_type=jnp.float32
            ).astype(jnp.bfloat16).astype(jnp.float32)
            block = piece if block is None else block + piece
        obuf[i] = block.astype(obuf.dtype)
        at = pl.multiple_of(j * rows, rows)
        pltpu.make_async_copy(obuf.at[i], out_ref.at[:, pl.ds(at, rows)], out_s.at[i]).start()

    for b in range(n):
        zb, same = b // 2, (b % 2) == x

        @pl.when(same & has_up & (zb <= z))
        def _(b=b):
            kv_copy(b, kvu_s, up).wait_send()
            for p in range(PIECES):
                w_copy(b, p, wu_s, up).wait_send()

        @pl.when(same & ((zb < z) | ((zb == z) & (x == 0))))
        def _(b=b):
            kv_copy(b, kvx_s, side).wait_send()

        @pl.when(same & has_down & (zb >= z))
        def _(b=b):
            for p in range(PIECES):
                w_copy(b, p, wd_s, down).wait_send()
            for p in range(PIECES):
                far_copy(b, p).wait_send()

        @pl.when(same & ((z < nz - 1) | (zb > 0)))
        def _(b=b):
            for p in range(PIECES):
                w_copy(b, p, wx_s, side).wait_send()

        if zb == 0:
            @pl.when(jnp.logical_not(same) & (z == nz - 2))
            def _(b=b):
                for p in range(PIECES):
                    w_copy(b, p, wu_s, up).wait_send()

        @pl.when((c != b) & jnp.logical_not(same & (zb > z)))
        def _(b=b):
            for p in range(PIECES):
                y_copy(b, p, lo).wait_send()

    for j in range(nh):
        for which in range(2):
            for p in range(PIECES):
                swap_copy((1 - h) * nh + j, which, p).wait_send()
        pltpu.make_async_copy(obuf.at[j], out_ref.at[:, pl.ds(j * rows, rows)], out_s.at[j]).wait()


def fused(queries, keys, values, lambda_vectors, out_weight, local_len, stride_keys, global_blocks):
    n = lax.axis_size("ctx")
    tok, _, width = queries.shape
    rows = out_weight.shape[0]
    nh = n // 2
    vmem = pl.BlockSpec(memory_space=pltpu.VMEM)
    smem = pl.BlockSpec(memory_space=pltpu.SMEM)
    hbm = pl.BlockSpec(memory_space=pl.ANY)
    dma = pltpu.SemaphoreType.DMA
    bf16 = jnp.bfloat16
    return pl.pallas_call(
        functools.partial(kernel, n),
        out_shape=jax.ShapeDtypeStruct((tok, nh * rows), bf16),
        in_specs=[hbm, hbm, hbm, hbm, vmem, smem, smem, smem],
        out_specs=hbm,
        scratch_shapes=[
            pltpu.VMEM((tok, width), bf16),
            pltpu.VMEM((n, 2, tok, width), bf16),
            pltpu.VMEM((n, rows, width), bf16),
            pltpu.VMEM((nh, rows, width), bf16),
            pltpu.VMEM((2, tok, n * tok), jnp.float32),
            pltpu.VMEM((tok, n * tok), bf16),
            pltpu.VMEM((tok, width), bf16),
            pltpu.VMEM((tok, width), bf16),
            pltpu.VMEM((nh, tok, rows), bf16),
        ]
        + [dma((n,))] * 3
        + [dma((n, PIECES))] * 7
        + [dma((n, PIECES))] * 2
        + [dma, dma, dma((4,)), dma((nh,))],
        compiler_params=pltpu.CompilerParams(
            collective_id=0, has_side_effects=True, vmem_limit_bytes=60 * 2**20
        ),
    )(
        queries.reshape(tok, width), keys.reshape(tok, width), values.reshape(tok, width),
        out_weight, lambda_vectors, local_len, stride_keys, global_blocks,
    )


def solution(mesh):
    in_specs = (
        P(("groups", "ctx"), "head", None),
        P(("groups", "ctx"), "head", None),
        P(("groups", "ctx"), "head", None),
        P(None, "head", None),
        P("ctx", "head"),
        P(("groups", "ctx")),
        P(("groups", "ctx"), None),
        P("groups"),
    )
    out_specs = P(("groups", "ctx"), "head")
    shape = mesh.shape

    def layer(queries, *rest):
        per_device = queries.shape[0] // (shape["groups"] * shape["ctx"])
        score_bytes = 8 * per_device * per_device * shape["ctx"]
        fits = score_bytes <= 8 * 2**20 and shape["groups"] == 2 and shape["head"] == 2
        chosen = fused if fits and shape["ctx"] % 4 == 0 else body
        mapped = jax.shard_map(chosen, mesh=mesh, in_specs=in_specs, out_specs=out_specs, check_vma=False)
        return mapped(queries, *rest)

    return layer
```

```python
import functools
import math

import jax
import jax.numpy as jnp
from jax import lax
from jax.experimental import pallas as pl
from jax.experimental.pallas import tpu as pltpu
from jax.sharding import PartitionSpec as P

BLK = 128
NSTR = 3
GLOB = 4
PIECES = 2
LAYER = 12


def shifted(shard, axis, by):
    length = lax.axis_size(axis)
    pairs = [(i, i + by) for i in range(length) if 0 <= i + by < length]
    return lax.ppermute(shard, axis, pairs)


def from_root(value, axis, source):
    kept = jnp.where(lax.axis_index(axis) == source, value, 0).astype(value.dtype)
    return lax.psum(kept, axis)


def masked_softmax(scores, allowed):
    masked_scores = jnp.where(allowed, scores, -jnp.inf)
    highest = jnp.max(masked_scores, -1, keepdims=True)
    raised = jnp.where(allowed, jnp.exp(masked_scores - highest), 0.0)
    return raised / jnp.sum(raised, -1, keepdims=True)


def body(queries, keys, values, lambda_vectors, out_weight, local_len, stride_keys, global_blocks):
    tok_dev, heads_here, double_width = queries.shape
    head_dim = double_width // 2
    blocks_here = tok_dev // BLK
    ctx_count = lax.axis_size("ctx")
    ctx_pos = lax.axis_index("ctx")
    step_dev = ctx_count // (NSTR + 1)
    lam_init = 0.8 - 0.6 * math.exp(-0.3 * (LAYER - 1))
    mixing = (
        jnp.exp(jnp.sum(lambda_vectors[0] * lambda_vectors[1], -1))
        - jnp.exp(jnp.sum(lambda_vectors[2] * lambda_vectors[3], -1))
        + lam_init
    )
    key_vals = jnp.concatenate((keys, values), axis=-1)
    prev_data = shifted(key_vals, "ctx", 1)
    remote = []
    moving = key_vals
    for slot_pos in range(NSTR):
        moving = shifted(moving, "ctx", step_dev)
        remote.append(moving)
    global_list = []
    for global_pos in range(GLOB):
        block_id = global_blocks[global_pos]
        owner_pos = block_id // blocks_here
        first_row = block_id % blocks_here * BLK
        block_data = lax.dynamic_slice_in_dim(key_vals, first_row, BLK, 0)
        global_list.append(from_root(block_data, "ctx", owner_pos))
    global_data = jnp.concatenate(global_list, 0)
    candidates = jnp.concatenate([key_vals, prev_data] + remote + [global_data], 0)
    cand_keys = candidates[..., :double_width]
    cand_values = candidates[..., double_width:]
    rows_here = jnp.arange(tok_dev, dtype=jnp.int32)
    query_pos = ctx_pos * tok_dev + rows_here
    query_block = query_pos // BLK
    owner_mask = (rows_here // BLK)[:, None] == jnp.arange(blocks_here, dtype=jnp.int32)[None, :]
    length = jnp.sum(jnp.where(owner_mask, local_len[None, :], 0), 1)
    stride_rows = jnp.sum(jnp.where(owner_mask[:, :, None], stride_keys[None, :, :], 0), 1)
    window_floor = query_block - length
    own_block = ctx_pos * blocks_here + rows_here // BLK
    own_ok = (own_block[None, :] > window_floor[:, None]) & (
        query_pos[None, :] - rows_here[:, None] + rows_here[None, :] <= query_pos[:, None]
    )
    prev_block = (ctx_pos - 1) * blocks_here + rows_here // BLK
    prev_ok = (prev_block[None, :] > window_floor[:, None]) & (prev_block[None, :] >= 0)
    masks = [own_ok, prev_ok]
    for slot_pos in range(NSTR):
        far_block = (ctx_pos - (slot_pos + 1) * step_dev) * blocks_here + rows_here // BLK
        listed = stride_rows[:, slot_pos][:, None]
        masks.append((listed == far_block[None, :]) & (listed >= 0))
    in_stride = jnp.any(stride_rows[:, :, None] == global_blocks[None, None, :], 1)
    global_key = jnp.repeat(global_blocks, BLK)
    global_ok = (global_key[None, :] <= window_floor[:, None]) & jnp.logical_not(
        jnp.repeat(in_stride, BLK, axis=1)
    )
    masks.append(global_ok)
    allowed = jnp.concatenate(masks, 1)
    score_scale = 1.0 / math.sqrt(head_dim)
    scores_one = (
        jnp.einsum(
            "qhd,khd->hqk",
            queries[..., :head_dim],
            cand_keys[..., :head_dim],
            preferred_element_type=jnp.float32,
        )
        * score_scale
    )
    scores_two = (
        jnp.einsum(
            "qhd,khd->hqk",
            queries[..., head_dim:],
            cand_keys[..., head_dim:],
            preferred_element_type=jnp.float32,
        )
        * score_scale
    )
    attn_one = masked_softmax(scores_one, allowed)
    attn_two = masked_softmax(scores_two, allowed)
    weights = (attn_one - mixing[:, None, None] * attn_two).astype(jnp.bfloat16)
    mixed_out = jnp.einsum("hqk,khe->qhe", weights, cand_values, preferred_element_type=jnp.float32)
    normed = (
        mixed_out
        * lax.rsqrt(jnp.mean(mixed_out * mixed_out, -1, keepdims=True) + 1e-05)
        * (1.0 - lam_init)
    ).astype(jnp.bfloat16)
    flat_heads = normed.reshape(tok_dev, heads_here * double_width)
    partials = lax.dot_general(
        flat_heads,
        lax.all_gather(out_weight, "ctx", axis=0, tiled=True),
        (((1,), (1,)), ((), ())),
        preferred_element_type=jnp.float32,
    )
    return lax.psum_scatter(partials.astype(jnp.bfloat16), "head", scatter_dimension=1, tiled=True)


MESH_ID = pl.DeviceIdType.MESH
MASKED = -1e30


def kernel(
    n, q_hbm, k_ref, v_ref, w_ref, lam_ref, len_ref, stride_ref, glob_ref, out_ref,
    q_ref, kv, wown, wother, scores, probs, mine, theirs, obuf,
    kvu_s, kvx_s, kv_r, wu_s, wd_s, wf_s, wx_s, w_r, wy_s, wy_r, sw_s, sw_r, nm_s, nm_r, loc, out_s,
):
    tok, width = q_ref.shape
    dh = width // 2
    rows = w_ref.shape[0]
    half = rows // 2
    size = half // PIECES
    nz, nh = n // 2, n // 2
    y, c, h = lax.axis_index("groups"), lax.axis_index("ctx"), lax.axis_index("head")
    z, x = c // 2, c % 2
    has_up, has_down = z + 1 < nz, z >= 1
    up, down, side = {"ctx": c + 2}, {"ctx": c - 2}, {"ctx": c + 1 - 2 * x}
    twin, core = {"groups": 1 - y}, {"head": 1 - h}
    lo, hi = y, 1 - y

    def rows_of(which, p):
        return pl.ds(pl.multiple_of(which * half + p * size, size), size)

    barrier = pltpu.get_barrier_semaphore()
    for to in (side, twin, core):
        pl.semaphore_signal(barrier, inc=1, device_id=to, device_id_type=MESH_ID)

    @pl.when(has_up)
    def _():
        pl.semaphore_signal(barrier, inc=1, device_id=up, device_id_type=MESH_ID)

    @pl.when(has_down)
    def _():
        pl.semaphore_signal(barrier, inc=1, device_id=down, device_id_type=MESH_ID)

    loads = [
        pltpu.make_async_copy(src, dst, loc.at[i])
        for i, (src, dst) in enumerate(
            ((k_ref, kv.at[c, 0]), (v_ref, kv.at[c, 1]), (w_ref, wown.at[c]), (q_hbm, q_ref))
        )
    ]
    for load in loads:
        load.start()
    pl.semaphore_wait(barrier, 3 + has_up.astype(jnp.int32) + has_down.astype(jnp.int32))

    def remote(src, dst, send, recv, to):
        return pltpu.make_async_remote_copy(
            src_ref=src, dst_ref=dst, send_sem=send, recv_sem=recv, device_id=to, device_id_type=MESH_ID
        )

    def kv_copy(b, send, to):
        return remote(kv.at[b], kv.at[b], send.at[b], kv_r.at[b], to)

    def w_copy(b, p, send, to):
        piece = wown.at[b, rows_of(lo, p)]
        return remote(piece, piece, send.at[b, p], w_r.at[b, p], to)

    def y_copy(b, p, which):
        piece = wown.at[b, rows_of(which, p)]
        return remote(piece, piece, wy_s.at[b, p], wy_r.at[b, p], twin)

    def far_copy(b, p):
        piece = wown.at[b, rows_of(hi, p)]
        return remote(piece, piece, wf_s.at[b, p], wy_r.at[b, p], down)

    def swap_copy(b, which, p):
        slot = b % nh
        return remote(
            wown.at[b, rows_of(which, p)], wother.at[slot, rows_of(which, p)],
            sw_s.at[2 * slot + which, p], sw_r.at[2 * slot + which, p], core,
        )

    def swap(b, which, p):
        @pl.when(b // nh == 1 - h)
        def _():
            swap_copy(b, which, p).start()

    def kv_up(d):
        @pl.when(z >= d)
        def _():
            b = c - 2 * d
            kv_copy(b, kvu_s, up).wait_recv()

            @pl.when(has_up)
            def _():
                kv_copy(b, kvu_s, up).start()

            kv_copy(b, kvx_s, side).start()

    def w_down(d):
        @pl.when(z + d < nz)
        def _():
            b = c + 2 * d
            for p in range(PIECES):
                w_copy(b, p, wd_s, down).wait_recv()

                @pl.when(has_down)
                def _():
                    w_copy(b, p, wd_s, down).start()

                w_copy(b, p, wx_s, side).start()
                swap(b, lo, p)

    def far_down(d):
        @pl.when(z + d < nz)
        def _():
            b = c + 2 * d
            for p in range(PIECES):
                far_copy(b, p).wait_recv()

                @pl.when(has_down)
                def _():
                    far_copy(b, p).start()

                swap(b, hi, p)

    def w_up(d):
        @pl.when(z >= d)
        def _():
            b = c - 2 * d
            for p in range(PIECES):
                w_copy(b, p, wu_s, up).wait_recv()

                @pl.when(has_up)
                def _():
                    w_copy(b, p, wu_s, up).start()

                y_copy(b, p, lo).start()
                if d < nz - 1:
                    w_copy(b, p, wx_s, side).start()
                swap(b, lo, p)

    def w_side(d):
        @pl.when((z + d < nz) & (z + d >= 0))
        def _():
            b = 2 * (z + d) + 1 - x
            for p in range(PIECES):
                w_copy(b, p, wx_s, side).wait_recv()
                y_copy(b, p, lo).start()
                if d == 2 - nz:
                    @pl.when(z == nz - 2)
                    def _():
                        w_copy(b, p, wu_s, up).start()

                swap(b, lo, p)

    def w_twin(b):
        for p in range(PIECES):
            y_copy(b, p, hi).wait_recv()
            swap(b, hi, p)

    def kv_side(d):
        @pl.when((z >= d) & ((d > 0) | (x == 1)))
        def _():
            b = 2 * (z - d) + 1 - x
            kv_copy(b, kvx_s, side).wait_recv()

    loads[2].wait()
    for p in range(PIECES):
        @pl.when(has_up)
        def _():
            w_copy(c, p, wu_s, up).start()

        w_copy(c, p, wx_s, side).start()

        @pl.when(has_down)
        def _():
            w_copy(c, p, wd_s, down).start()

    loads[0].wait()
    loads[1].wait()

    @pl.when(has_up)
    def _():
        kv_copy(c, kvu_s, up).start()

    @pl.when(x == 0)
    def _():
        kv_copy(c, kvx_s, side).start()

    for p in range(PIECES):
        @pl.when(has_down)
        def _():
            far_copy(c, p).start()

        swap(c, 0, p)
        swap(c, 1, p)

    for b in range(1, n):
        @pl.when(c < b)
        def _(b=b):
            kv[b] = jnp.zeros(kv.shape[1:], kv.dtype)

    for d in range(1, nz):
        w_down(d)
        w_up(d)
        w_side(d - 1)
        if d > 1:
            w_side(1 - d)
        kv_up(d)
        far_down(d)

    scale = 1.0 / math.sqrt(dh)
    lam_init = 0.8 - 0.6 * math.exp(-0.3 * (LAYER - 1))
    lam = [lam_ref[i] for i in range(4)]
    mixing = (
        jnp.exp(jnp.sum(lam[0] * lam[1], -1, keepdims=True))
        - jnp.exp(jnp.sum(lam[2] * lam[3], -1, keepdims=True))
        + lam_init
    )
    blocks_here = tok // BLK

    def score(m):
        q = q_ref[:, m * dh : (m + 1) * dh]
        for b in range(n):
            scores[m, :, b * tok : (b + 1) * tok] = lax.dot_general(
                q, kv[b, 0, :, m * dh : (m + 1) * dh], (((1,), (1,)), ((), ())),
                preferred_element_type=jnp.float32,
            ) * scale

    part = 64

    def soften(i, carry):
        at = pl.multiple_of(i * part, part)
        key_pos = lax.broadcasted_iota(jnp.int32, (1, n * tok), 1)
        key_block = key_pos // BLK
        which = i // (BLK // part)
        block = c * blocks_here + which
        length = len_ref[0]
        stride = [stride_ref[0, j] for j in range(NSTR)]
        for g in range(1, blocks_here):
            length = jnp.where(which == g, len_ref[g], length)
            stride = [jnp.where(which == g, stride_ref[g, j], stride[j]) for j in range(NSTR)]
        floor = block - length
        ok = key_block > floor
        for j in range(NSTR):
            ok = ok | (key_block == stride[j])
        for j in range(GLOB):
            g = glob_ref[j]
            ok = ok | ((key_block == g) & (key_block <= floor))
        last = jnp.where(ok, key_pos, n * tok)
        query = c * tok + at + lax.broadcasted_iota(jnp.int32, (part, 1), 0)
        allowed = last <= query
        maps = []
        for m in range(2):
            s = jnp.where(allowed, scores[m, pl.ds(at, part), :], MASKED)
            e = jnp.exp(s - jnp.max(s, -1, keepdims=True))
            maps.append((e, 1.0 / jnp.sum(e, -1, keepdims=True)))
        (e1, r1), (e2, r2) = maps
        probs[pl.ds(at, part), :] = (e1 * r1 - e2 * (mixing * r2)).astype(probs.dtype)
        return carry

    chunks = tok // part
    w_side(nz - 1)
    for far in range(nz):
        kv_side(far)
    loads[3].wait()
    score(0)
    score(1)
    for i in range(chunks):
        soften(i, 0)
        if i == 0:
            w_side(1 - nz)
    mixed = jnp.zeros((tok, width), jnp.float32)
    for b in range(n):
        mixed = mixed + jnp.dot(
            probs[:, b * tok : (b + 1) * tok], kv[b, 1], preferred_element_type=jnp.float32
        )
    normed = mixed * lax.rsqrt(jnp.mean(mixed * mixed, -1, keepdims=True) + 1e-05) * (1.0 - lam_init)
    mine[...] = normed.astype(mine.dtype)
    trade = remote(mine, theirs, nm_s, nm_r, core)
    trade.start()

    def twin_at(d, here):
        @pl.when((z + d < nz) & (z + d >= 0))
        def _():
            w_twin(2 * (z + d) + (x if here else 1 - x))

    for d in range(1, nz):
        twin_at(-d, True)
        twin_at(d - 1, False)
        if d > 1:
            twin_at(1 - d, False)
    trade.wait()

    for i in range(nh):
        if i == nh - 1:
            twin_at(nz - 1, False)
            twin_at(1 - nz, False)
        pair = jnp.where(z >= nz // 2, nh // 2 - 1 - i // 2, i // 2)
        j = 2 * pair + (x if i % 2 == 0 else 1 - x)
        for which in range(2):
            for p in range(PIECES):
                swap_copy(h * nh + j, which, p).wait_recv()
        block = None
        for left, weight in ((mine, wown.at[h * nh + j]), (theirs, wother.at[j])):
            piece = lax.dot_general(
                left[...], weight[...], (((1,), (1,)), ((), ())), preferred_element_type=jnp.float32
            ).astype(jnp.bfloat16).astype(jnp.float32)
            block = piece if block is None else block + piece
        obuf[i] = block.astype(obuf.dtype)
        at = pl.multiple_of(j * rows, rows)
        pltpu.make_async_copy(obuf.at[i], out_ref.at[:, pl.ds(at, rows)], out_s.at[i]).start()

    for b in range(n):
        zb, same = b // 2, (b % 2) == x

        @pl.when(same & has_up & (zb <= z))
        def _(b=b):
            kv_copy(b, kvu_s, up).wait_send()
            for p in range(PIECES):
                w_copy(b, p, wu_s, up).wait_send()

        @pl.when(same & ((zb < z) | ((zb == z) & (x == 0))))
        def _(b=b):
            kv_copy(b, kvx_s, side).wait_send()

        @pl.when(same & has_down & (zb >= z))
        def _(b=b):
            for p in range(PIECES):
                w_copy(b, p, wd_s, down).wait_send()
            for p in range(PIECES):
                far_copy(b, p).wait_send()

        @pl.when(same & ((z < nz - 1) | (zb > 0)))
        def _(b=b):
            for p in range(PIECES):
                w_copy(b, p, wx_s, side).wait_send()

        if zb == 0:
            @pl.when(jnp.logical_not(same) & (z == nz - 2))
            def _(b=b):
                for p in range(PIECES):
                    w_copy(b, p, wu_s, up).wait_send()

        @pl.when((c != b) & jnp.logical_not(same & (zb > z)))
        def _(b=b):
            for p in range(PIECES):
                y_copy(b, p, lo).wait_send()

    for j in range(nh):
        for which in range(2):
            for p in range(PIECES):
                swap_copy((1 - h) * nh + j, which, p).wait_send()
        pltpu.make_async_copy(obuf.at[j], out_ref.at[:, pl.ds(j * rows, rows)], out_s.at[j]).wait()


def fused(queries, keys, values, lambda_vectors, out_weight, local_len, stride_keys, global_blocks):
    n = lax.axis_size("ctx")
    tok, _, width = queries.shape
    rows = out_weight.shape[0]
    nh = n // 2
    vmem = pl.BlockSpec(memory_space=pltpu.VMEM)
    smem = pl.BlockSpec(memory_space=pltpu.SMEM)
    hbm = pl.BlockSpec(memory_space=pl.ANY)
    dma = pltpu.SemaphoreType.DMA
    bf16 = jnp.bfloat16
    return pl.pallas_call(
        functools.partial(kernel, n),
        out_shape=jax.ShapeDtypeStruct((tok, nh * rows), bf16),
        in_specs=[hbm, hbm, hbm, hbm, vmem, smem, smem, smem],
        out_specs=hbm,
        scratch_shapes=[
            pltpu.VMEM((tok, width), bf16),
            pltpu.VMEM((n, 2, tok, width), bf16),
            pltpu.VMEM((n, rows, width), bf16),
            pltpu.VMEM((nh, rows, width), bf16),
            pltpu.VMEM((2, tok, n * tok), jnp.float32),
            pltpu.VMEM((tok, n * tok), bf16),
            pltpu.VMEM((tok, width), bf16),
            pltpu.VMEM((tok, width), bf16),
            pltpu.VMEM((nh, tok, rows), bf16),
        ]
        + [dma((n,))] * 3
        + [dma((n, PIECES))] * 7
        + [dma((n, PIECES))] * 2
        + [dma, dma, dma((4,)), dma((nh,))],
        compiler_params=pltpu.CompilerParams(
            collective_id=0, has_side_effects=True, vmem_limit_bytes=60 * 2**20
        ),
    )(
        queries.reshape(tok, width), keys.reshape(tok, width), values.reshape(tok, width),
        out_weight, lambda_vectors, local_len, stride_keys, global_blocks,
    )


def solution(mesh):
    in_specs = (
        P(("groups", "ctx"), "head", None),
        P(("groups", "ctx"), "head", None),
        P(("groups", "ctx"), "head", None),
        P(None, "head", None),
        P("ctx", "head"),
        P(("groups", "ctx")),
        P(("groups", "ctx"), None),
        P("groups"),
    )
    out_specs = P(("groups", "ctx"), "head")
    shape = mesh.shape

    def layer(queries, *rest):
        per_device = queries.shape[0] // (shape["groups"] * shape["ctx"])
        score_bytes = 8 * per_device * per_device * shape["ctx"]
        fits = score_bytes <= 8 * 2**20 and shape["groups"] == 2 and shape["head"] == 2
        chosen = fused if fits and shape["ctx"] % 4 == 0 else body
        mapped = jax.shard_map(chosen, mesh=mesh, in_specs=in_specs, out_specs=out_specs, check_vma=False)
        return mapped(queries, *rest)

    return layer
```
